512 devices in a mesh: ctx: 64 (over x, z), head: 8 (over y, core).
Axes of the slice: x: 4, y: 4, z: 16, core: 2. Of those that a mesh axis runs over, the one named last changes fastest.
Arguments:
- queries: bfloat16 [8192, 8192], P('ctx', 'head'), may hold values from -8 to 8
- keys: bfloat16 [8192, 1024], P('ctx', 'head'), may hold values from -8 to 8
- values: bfloat16 [8192, 1024], P('ctx', 'head'), may hold values from -12 to 12
- tile_mask: int32 [8, 64, 64], P('head'), may hold values from 0 to 1, as said below
Outputs:
- attn_out: bfloat16 [8192, 8192], P('ctx', 'head')
- key_coeffs: float32 [8192, 160], P('ctx')
- key_factor: float32 [160, 1024], P(None, 'head')
The draws below stay inside these ranges and needn't reach their ends.
Inputs may be any that keep to these rules, and one draw needn't show every extreme that they name: tile_mask[h, i, j] is 1 exactly where j <= i and either j is one of 4 vertical tiles of head h (tile 0 among them) or i - j is one of 4 diagonal offsets of head h (offset 0 among them).
All inputs are finite; a program needn't handle non-finite values.
Results may differ from the reference program's by a relative error of at most 0.011.
Values may be sent and summed in bfloat16 or wider, within the bound.
No kernel may reach another device: no remote copies, remote signals or barrier semaphores. Data moves between devices by JAX's collectives and lax.ppermute only.
A program may use at most 64 MiB of HBM per device.

```python
import math
import jax
import jax.numpy as jnp
from jax import lax

HD = 128
KVH = 8
GQ = 8
RANK = 160
TILE = 128
VT = 4
SL = 4
PIVOTS = 20
TOKENS = 8192
NT = 64


def draw_queries(key, part):
    key = jax.random.fold_in(key, 1)
    result = jnp.clip(1.5 * jax.random.normal(key, (TOKENS, KVH, GQ, HD), jnp.float32), -8.0, 8.0)
    return result.reshape(TOKENS, KVH * GQ * HD).astype(jnp.bfloat16)


def draw_keys(key, part):
    key = jax.random.fold_in(key, 2)
    result = jnp.clip(1.5 * jax.random.normal(key, (TOKENS, KVH, HD), jnp.float32), -8.0, 8.0)
    return result.reshape(TOKENS, KVH * HD).astype(jnp.bfloat16)


def draw_tile_mask(key, part):
    key = jax.random.fold_in(key, 3)

    def head_mask(head_key):
        key_vert, key_slant = jax.random.split(head_key)
        vertical = jnp.concatenate([jnp.zeros((1,), jnp.int32), jax.random.permutation(key_vert, NT - 1)[:VT - 1].astype(jnp.int32) + 1])
        slanted = jnp.concatenate([jnp.zeros((1,), jnp.int32), jax.random.permutation(key_slant, NT - 1)[:SL - 1].astype(jnp.int32) + 1])
        columns = jnp.arange(NT, dtype=jnp.int32)
        vert_flag = jnp.any(vertical[:, None] == columns[None, :], axis=0)
        slant_flag = jnp.any(slanted[:, None] == columns[None, :], axis=0)
        distance = jnp.clip(columns[:, None] - columns[None, :], 0, NT - 1)
        chosen = (columns[None, :] <= columns[:, None]) & (vert_flag[None, :] | slant_flag[distance])
        return chosen.astype(jnp.int32)
    return jax.vmap(head_mask)(jax.random.split(key, KVH))


def shard_levels(own_key, extent, shards, least, largest):
    factor_of, own = 1.0, jax.random.fold_in(own_key, 6)
    for dim, blocks in shards:
        heights = jnp.exp(jax.random.uniform(jax.random.fold_in(own, dim), (blocks,), jnp.float32, least / len(shards), largest / len(shards)))
        factor_of = factor_of * jnp.repeat(heights, extent[dim] // blocks).reshape([-1 if axis == dim else 1 for axis in range(len(extent))])
    return factor_of


def normal_values(own_key, extent, scale, limit, pieces=(), kind=jnp.bfloat16):
    drawn = scale * jax.random.normal(own_key, extent, jnp.float32)
    if pieces:
        drawn = drawn * shard_levels(own_key, extent, pieces, -0.22, 0.18)
    return jnp.clip(drawn, -limit, limit).astype(kind)


def setup_inputs(seed: int = 0) -> dict:
    arg_keys = jax.random.split(jax.random.key(seed), 5)
    queries = draw_queries(jax.random.fold_in(arg_keys[4], 71), 0)
    keys = draw_keys(jax.random.fold_in(arg_keys[4], 71), 0)
    values = normal_values(arg_keys[2], (TOKENS, KVH * HD), 3.0, 12.0, ((0, 64), (1, 8)))
    tile_mask = draw_tile_mask(jax.random.fold_in(arg_keys[4], 71), 0)
    return dict(queries=queries, keys=keys, values=values, tile_mask=tile_mask)


NEG = -1e+30
ROPE_BASE = 500000.0

def angles(positions, width):
    inverse = jnp.exp(-math.log(ROPE_BASE) * 2.0 * jnp.arange(width // 2, dtype=jnp.float32) / width)
    turning = positions[:, None] * inverse[None, :]
    turning = jnp.concatenate([turning, turning], axis=1)
    return (jnp.cos(turning), jnp.sin(turning))

def rotate(head_vals, cosine, sine):
    shape = (cosine.shape[0],) + (1,) * (head_vals.ndim - 2) + (cosine.shape[1],)
    half_size = head_vals.shape[-1] // 2
    turned = jnp.concatenate([-head_vals[..., half_size:], head_vals[..., :half_size]], axis=-1)
    return head_vals * cosine.reshape(shape) + turned * sine.reshape(shape)

def reference(queries, keys, values, tile_mask):
    positions = jnp.arange(TOKENS, dtype=jnp.float32)
    cosine, sine = angles(positions, HD)
    rot_queries = rotate(queries.reshape(TOKENS, KVH, GQ, HD).astype(jnp.float32), cosine, sine).astype(jnp.bfloat16)
    rot_keys = rotate(keys.reshape(TOKENS, KVH, HD).astype(jnp.float32), cosine, sine).astype(jnp.bfloat16)
    query_tiles = rot_queries.reshape(NT, TILE, KVH, GQ, HD)
    key_tiles = rot_keys.reshape(NT, TILE, KVH, HD).transpose(2, 0, 1, 3)
    value_tiles = values.reshape(NT, TILE, KVH, HD).transpose(2, 0, 1, 3)
    tile_count = min(VT + SL, NT)
    offsets = jnp.arange(TILE, dtype=jnp.int32)
    score_scale = HD ** (-0.5)

    def attend_tile(flat_index):
        head_index = flat_index // NT
        tile_row = flat_index % NT
        mask_line = tile_mask[head_index, tile_row]
        ranking = mask_line * (2 * NT) + jnp.arange(NT, dtype=jnp.int32)
        unused, picked = lax.top_k(ranking, tile_count)
        usable = jnp.take(mask_line, picked) == 1
        key_block = key_tiles[head_index][picked]
        value_block = value_tiles[head_index][picked]
        query_block = query_tiles[tile_row][:, head_index]
        query_pos = tile_row * TILE + offsets
        key_pos = picked[:, None] * TILE + offsets[None, :]
        allowed = usable[None, :, None] & (key_pos[None, :, :] <= query_pos[:, None, None])
        scores = jnp.einsum('rgd,ktd->grkt', query_block.astype(jnp.float32), key_block.astype(jnp.float32)) * score_scale
        scores = jnp.where(allowed[None], scores, NEG)
        row_max = jnp.max(scores, axis=(2, 3))
        weights = jnp.where(allowed[None], jnp.exp(scores - row_max[:, :, None, None]), 0.0)
        totals = jnp.sum(weights, axis=(2, 3))
        rounded = lax.optimization_barrier(weights.astype(jnp.bfloat16)).astype(jnp.float32)
        mixed = jnp.einsum('grkt,ktd->rgd', rounded, value_block.astype(jnp.float32))
        return (mixed / totals.T[:, :, None]).astype(jnp.bfloat16)
    blocks = lax.map(attend_tile, jnp.arange(KVH * NT, dtype=jnp.int32))
    attn_out = blocks.reshape(KVH, NT, TILE, GQ, HD).transpose(1, 2, 0, 3, 4).reshape(TOKENS, KVH * GQ * HD)
    pivots = keys.reshape(TOKENS, KVH, HD)[:, :, :PIVOTS].reshape(TOKENS, RANK)
    gram_sum = jnp.dot(pivots.T.astype(jnp.float32), pivots.astype(jnp.float32), preferred_element_type=jnp.float32)
    cross_sum = jnp.dot(pivots.T.astype(jnp.float32), keys.astype(jnp.float32), preferred_element_type=jnp.float32)
    lower_factor = jnp.linalg.cholesky(gram_sum / TOKENS)
    key_factor = jax.scipy.linalg.solve_triangular(lower_factor, cross_sum / TOKENS, lower=True)
    key_coeffs = jax.scipy.linalg.solve_triangular(lower_factor, pivots.astype(jnp.float32).T, lower=True).T
    return (attn_out, key_coeffs, key_factor)
```

```python
import functools
import math

import jax
import jax.numpy as jnp
from jax import lax
from jax.experimental import pallas as pl
from jax.experimental.pallas import tpu as pltpu
from jax.sharding import PartitionSpec as P

HD = 128
GQ = 8
TILE = 128
PIVOTS = 20
NEAR = 4
FAR = 4
PANEL = 40
STRIP = 8
PIECE = 16
UNIT = 16
SLOTS = 7
NEG = -1e30
ROPE_BASE = 500000.0
VMEM_LIMIT = 48 * 1024 * 1024


def angles(positions, width):
    inverse = jnp.exp(
        -math.log(ROPE_BASE) * 2.0 * jnp.arange(width // 2, dtype=jnp.float32) / width
    )
    turning = positions[:, None] * inverse[None, :]
    cosine, sine = jnp.cos(turning), jnp.sin(turning)
    return (
        jnp.concatenate([cosine, cosine], axis=1),
        jnp.concatenate([-sine, sine], axis=1),
    )


def turn(head_vals, cosine, signed_sine):
    return head_vals * cosine + pltpu.roll(head_vals, HD // 2, 1) * signed_sine


def params():
    return pltpu.CompilerParams(vmem_limit_bytes=VMEM_LIMIT)


def iota(shape, dim):
    return lax.broadcasted_iota(jnp.int32, shape, dim)


def pivots_kernel(keys_ref, piv_ref):
    first = (iota((32, HD), 0) == iota((32, HD), 1)).astype(jnp.bfloat16)
    pivots = lax.dot_general(
        first, keys_ref[...], (((1,), (1,)), ((), ())), preferred_element_type=jnp.float32
    ).astype(jnp.bfloat16)
    for head in range(piv_ref.shape[0]):
        piv_ref[head] = pivots


def prepare_kernel(keys_ref, values_ref, cos_ref, sin_ref, kv_ref):
    keys = keys_ref[...].astype(jnp.float32)
    kv_ref[0:TILE, :] = turn(keys, cos_ref[...], sin_ref[...]).astype(jnp.bfloat16)
    kv_ref[TILE:, :] = values_ref[...]


def queries_kernel(me_ref, mask_ref, queries_ref, cos_ref, sin_ref, out_ref, bias_ref):
    cosine, sine = cos_ref[...], sin_ref[...]
    for g in range(GQ):
        lanes = slice(g * HD, (g + 1) * HD)
        query = turn(queries_ref[:, lanes].astype(jnp.float32), cosine, sine)
        out_ref[:, lanes] = query.astype(jnp.bfloat16)
    mask = mask_ref[0]
    count = jnp.sum(jnp.where(iota(mask.shape, 0) == me_ref[0], mask, 0)) - 1
    width = SLOTS * TILE
    slot = iota((TILE, width), 1) % (SLOTS * PIECE) // PIECE
    bias_ref[:, 0:width] = jnp.where(slot < count, 0.0, NEG)
    below = iota((TILE, TILE), 1) <= iota((TILE, TILE), 0)
    bias_ref[:, width:] = jnp.where(below, 0.0, NEG)


def index_kernel(stride, far_ref, mask_ref, out_ref):
    tiles = mask_ref.shape[1]
    dests = out_ref.shape[0]
    mask = mask_ref[0].astype(jnp.bfloat16)
    dest = iota((dests, tiles), 0)
    tile = dest // NEAR * FAR * NEAR + far_ref[0] * NEAR + dest % NEAR
    own = (tile == iota((dests, tiles), 1)).astype(jnp.bfloat16)
    mine = jnp.dot(own, mask, preferred_element_type=jnp.float32)
    mine = mine * (1.0 - own.astype(jnp.float32))
    before = (iota((tiles, tiles), 0) < iota((tiles, tiles), 1)).astype(jnp.bfloat16)
    rank = jnp.dot(mine.astype(jnp.bfloat16), before, preferred_element_type=jnp.float32)
    col = iota((dests, tiles), 1)
    place = col // NEAR % FAR * stride + (col // (FAR * NEAR) * NEAR + col % NEAR) * PIECE
    place = place.astype(jnp.float32) * mine
    lane = iota(out_ref.shape, 1)
    found = jnp.zeros(out_ref.shape, jnp.float32)
    for slot in range(SLOTS):
        value = jnp.sum(jnp.where(rank == slot, place, 0.0), axis=1, keepdims=True)
        found = jnp.where(lane == slot, value, found)
    out_ref[...] = found.astype(jnp.int32)


def two_terms(total):
    high = total.astype(jnp.bfloat16).astype(jnp.float32)
    return jnp.concatenate([high, total - high], axis=0).astype(jnp.bfloat16)


def one_term(terms):
    terms = terms.astype(jnp.float32)
    half = terms.shape[0] // 2
    return terms[0:half] + terms[half:]


def fold(cross, gram, all_ref):
    rank, half = gram.shape[0], 64
    rest = rank - 128
    row, lane = iota((half, 128), 0), iota((half, 128), 1)
    low = gram[half:128, 0:128]
    diagonal = jnp.sum(jnp.where(lane == row + half, low, 0.0), axis=1, keepdims=True)
    corner = jnp.concatenate(
        [gram[128:, 128:], jnp.zeros((rest, 128 - rest), jnp.float32)], axis=1
    )
    hidden = jnp.concatenate(
        [
            corner,
            pltpu.roll(corner, 128 - rest // 2, 1),
            jnp.broadcast_to(diagonal, (half, 128)),
            jnp.zeros((rank - 2 * rest - half, 128), jnp.float32),
        ],
        axis=0,
    )
    all_ref[0:rank, :] = jnp.where(iota((rank, 128), 1) < PIVOTS, hidden, cross)
    keep = (lane < half) & (lane <= row)
    all_ref[rank:rank + half, :] = jnp.where(keep, gram[0:half, 0:128], pltpu.roll(low, half, 1))
    all_ref[rank + half:, :] = gram[128:, 0:128]


def unfold(head, inverse, sums_ref, work_ref):
    rank, half = work_ref.shape[0], 64
    rest = rank - 128
    row, lane = iota((half, 128), 0), iota((half, 128), 1)
    mixed = sums_ref[rank:rank + half, :] * inverse
    turned = pltpu.roll(mixed, half, 1)
    diagonal = jnp.broadcast_to(sums_ref[2 * rest:2 * rest + half, 0:1], (half, 128)) * inverse
    top = jnp.where((lane < half) & (lane <= row), mixed, 0.0)
    low = jnp.where(
        (lane < half) | (lane > row + half), turned, jnp.where(lane == row + half, diagonal, 0.0)
    )
    one_side = jnp.concatenate([top, low], axis=0)
    other = jnp.where(iota((128, 128), 0) == iota((128, 128), 1), 0.0, one_side.T)
    work_ref[0:128, 0:128] = one_side + other
    last = sums_ref[rank + half:, :] * inverse
    work_ref[128:, 0:128] = last
    work_ref[0:128, 128:256] = jnp.concatenate(
        [last, jnp.zeros((128 - rest, 128), jnp.float32)], axis=0
    ).T
    lane = iota((rest, 128), 1)
    second = pltpu.roll(sums_ref[rest:2 * rest, :], rest // 2, 1)
    corner = jnp.where(lane < rest // 2, sums_ref[0:rest, :], second)
    work_ref[128:, 128:256] = jnp.where(lane < rest, corner * inverse, 0.0)
    own = pltpu.roll(work_ref[:, 0:256], 256 - head * PIVOTS, 1)[:, 0:128]
    work_ref[:, 256:384] = jnp.where(
        iota((rank, 128), 1) < PIVOTS, own, sums_ref[0:rank, :] * inverse
    )


def sums_kernel(piv_ref, keys_ref, kv_ref, out_ref, pivt_ref, all_ref):
    heads = piv_ref.shape[0]
    rank = heads * PIVOTS
    padded = piv_ref[...].reshape(heads * 32, TILE)
    line = iota((rank, heads * 32), 0)
    place = line // PIVOTS * 32 + line % PIVOTS
    compact = (place == iota((rank, heads * 32), 1)).astype(jnp.bfloat16)
    pivt = jnp.dot(compact, padded, preferred_element_type=jnp.float32).astype(jnp.bfloat16)
    pivt_ref[...] = pivt
    cross = jnp.dot(pivt, keys_ref[...], preferred_element_type=jnp.float32)
    gram = lax.dot_general(
        pivt, pivt, (((1,), (1,)), ((), ())), preferred_element_type=jnp.float32
    )
    fold(cross, gram, all_ref)
    for dest in range(out_ref.shape[0]):
        out_ref[dest, 0:PIECE] = kv_ref[dest * PIECE:(dest + 1) * PIECE, :]
        out_ref[dest, PIECE:] = two_terms(all_ref[dest * UNIT:(dest + 1) * UNIT, :])


def middle_kernel(in_ref, out_ref):
    near = in_ref.shape[0]
    total = one_term(in_ref[0, PIECE:])
    for source in range(1, near):
        total = total + one_term(in_ref[source, PIECE:])
    terms = two_terms(total)
    for dest in range(out_ref.shape[0]):
        for source in range(near):
            out_ref[dest, source * PIECE:(source + 1) * PIECE] = in_ref[source, 0:PIECE]
        out_ref[dest, near * PIECE:] = terms


def pick_kernel(place_ref, in_ref, out_ref):
    near, stride = out_ref.shape[0], in_ref.shape[0] // FAR
    total = one_term(in_ref[near * PIECE:stride, :])
    for far in range(1, FAR):
        total = total + one_term(in_ref[far * stride + near * PIECE:(far + 1) * stride, :])
    terms = two_terms(total)
    for dest in range(near):
        for slot in range(SLOTS):
            start = pl.multiple_of(place_ref[dest, slot], PIECE)
            out_ref[dest, slot * PIECE:(slot + 1) * PIECE] = in_ref[pl.ds(start, PIECE), :]
        out_ref[dest, SLOTS * PIECE:] = terms


def basis_steps(tokens, head, in_ref, pivt_ref, factor_ref, coeffs_ref, work_ref, sums_ref):
    rank = pivt_ref.shape[0]
    for source in range(in_ref.shape[0]):
        sums_ref[source * UNIT:(source + 1) * UNIT, :] = one_term(in_ref[source, SLOTS * PIECE:])
    unfold(head, 1.0 / tokens, sums_ref, work_ref)
    work_ref[:, 384:512] = pivt_ref[...].astype(jnp.float32)
    for first in range(0, rank, PANEL):
        block = work_ref[first:first + PANEL, :]
        for start in range(first, first + PANEL, STRIP):
            height = block.shape[0]
            columns = [
                jnp.broadcast_to(block[:, at:at + 1], (height, 128))
                for at in range(start, start + STRIP)
            ]
            for step in range(STRIP):
                root = lax.rsqrt(columns[step][step:step + 1, :])
                column = columns[step] * root
                for later in range(step + 1, STRIP):
                    columns[later] = columns[later] - column * column[later:later + 1, :]
                line = block[step:step + 1, :] * jnp.concatenate([root] * 4, axis=1)
                work_ref[start + step:start + step + 1, :] = line
                block = block - jnp.concatenate([column] * 4, axis=1) * line
                yield
            block = block[STRIP:, :]
        last = first + PANEL
        if last < rank:
            done = work_ref[first:last, :]
            update = lax.dot_general(
                done[:, 0:256], done, (((0,), (0,)), ((), ())),
                precision=lax.Precision.HIGHEST, preferred_element_type=jnp.float32,
            )
            work_ref[last:rank, :] = work_ref[last:rank, :] - update[last:rank, :]
    factor_ref[...] = work_ref[:, 256:384]
    coeffs_ref[...] = work_ref[:, 384:512]


def attend_steps(queries_ref, bias_ref, in_ref, kv_ref, out_ref):
    per_dest = SLOTS * PIECE
    half = in_ref.shape[0] // 2
    width = half * per_dest
    keys = jnp.concatenate(
        [in_ref[0:half, 0:per_dest].reshape(width, HD), kv_ref[0:TILE, :]], axis=0
    )
    values = jnp.concatenate(
        [in_ref[half:, 0:per_dest].reshape(width, HD), kv_ref[TILE:, :]], axis=0
    )
    scale = HD ** (-0.5) * math.log2(math.e)
    for g in range(GQ):
        lanes = slice(g * HD, (g + 1) * HD)
        scores = lax.dot_general(
            queries_ref[:, lanes], keys, (((1,), (1,)), ((), ())),
            preferred_element_type=jnp.float32,
        ) * scale + bias_ref[...]
        yield
        most = jnp.max(scores, axis=1, keepdims=True)
        yield
        weights = jnp.exp2(scores - most)
        totals = jnp.sum(weights, axis=1, keepdims=True)
        yield
        mixed = jnp.dot(
            weights.astype(jnp.bfloat16), values, preferred_element_type=jnp.float32
        )
        yield
        out_ref[:, lanes] = (mixed / totals).astype(jnp.bfloat16)


def finish_kernel(
    tokens, head_ref, queries_ref, bias_ref, in_ref, kv_ref, pivt_ref,
    out_ref, factor_ref, coeffs_ref, work_ref, sums_ref,
):
    basis = basis_steps(
        tokens, head_ref[0], in_ref, pivt_ref, factor_ref, coeffs_ref, work_ref, sums_ref
    )
    attend = attend_steps(queries_ref, bias_ref, in_ref, kv_ref, out_ref)
    steps = pivt_ref.shape[0]
    for step in range(steps):
        next(basis, None)
        if step % (steps // (4 * GQ)) == 0:
            next(attend, None)
    for rest in (attend, basis):
        for _ in rest:
            pass


def on_device(queries, keys, values, tile_mask):
    near_axes = ("x", "near")
    near_size = lax.axis_size(near_axes)
    far_size = lax.axis_size("far")
    head_size = lax.axis_size("head")
    far_index = lax.axis_index("far")
    ctx_index = lax.axis_index(("x", "far", "near"))
    tok_rows = keys.shape[0]
    token_total = tok_rows * near_size * far_size
    rank = head_size * PIVOTS
    positions = ctx_index * tok_rows + lax.iota(jnp.int32, tok_rows)
    cosine, sine = angles(positions.astype(jnp.float32), HD)
    shape = jax.ShapeDtypeStruct
    bf16, f32 = jnp.bfloat16, jnp.float32
    smem, vmem = pl.BlockSpec(memory_space=pltpu.SMEM), pl.BlockSpec(memory_space=pltpu.VMEM)

    def call(kernel, name, out_shape, scalars, *arrays, scratch=()):
        return pl.pallas_call(
            kernel,
            out_shape=out_shape,
            in_specs=[smem] * scalars + [vmem] * (len(arrays) - scalars),
            scratch_shapes=scratch,
            compiler_params=params(),
            name=name,
        )(*arrays)

    pivots = call(pivots_kernel, "pivots", shape((head_size, 32, TILE), bf16), 0, keys)
    pivots = lax.all_to_all(pivots, "head", 0, 0)
    kv = call(
        prepare_kernel, "prepare", shape((2 * TILE, HD), bf16), 0, keys, values, cosine, sine
    )
    stride = near_size * PIECE + 2 * UNIT
    places = call(
        functools.partial(index_kernel, stride), "index",
        shape((near_size, 128), jnp.int32), 1, far_index.reshape(1), tile_mask,
    )
    turned, bias = call(
        queries_kernel, "queries",
        (shape(queries.shape, bf16), shape((TILE, (SLOTS + 1) * TILE), f32)), 1,
        ctx_index.reshape(1), tile_mask, queries, cosine, sine,
    )
    pivots, kv, places, turned, bias, head_index = lax.optimization_barrier(
        (pivots, kv, places, turned, bias, lax.axis_index("head").reshape(1))
    )
    first, pivt = call(
        sums_kernel, "sums",
        (shape((near_size, PIECE + 2 * UNIT, HD), bf16), shape((rank, TILE), bf16)), 0,
        pivots, keys, kv,
        scratch=[pltpu.VMEM((near_size * UNIT, HD), f32)],
    )
    first = lax.all_to_all(first, near_axes, 0, 0)
    second = call(middle_kernel, "middle", shape((far_size, stride, HD), bf16), 0, first)
    second = lax.all_to_all(second, "far", 0, 0)
    third = call(
        pick_kernel, "pick", shape((near_size, SLOTS * PIECE + 2 * UNIT, HD), bf16), 1,
        places, second.reshape(far_size * stride, HD),
    )
    third = lax.all_to_all(third, near_axes, 0, 0)

    attn_out, key_factor, coeffs = call(
        functools.partial(finish_kernel, float(token_total)), "finish",
        (shape(queries.shape, bf16), shape((rank, HD), f32), shape((rank, TILE), f32)), 1,
        head_index, turned, bias, third, kv, pivt,
        scratch=[pltpu.VMEM((rank, 512), f32), pltpu.VMEM((near_size * UNIT, HD), f32)],
    )
    return (attn_out, coeffs.T, key_factor)


def solution(mesh):
    ctx_size, head_size = mesh.shape["ctx"], mesh.shape["head"]
    split = jax.sharding.Mesh(
        mesh.devices.reshape(ctx_size // (FAR * NEAR), FAR, NEAR, head_size),
        ("x", "far", "near", "head"),
    )
    ctx = ("x", "far", "near")
    return jax.shard_map(
        on_device,
        mesh=split,
        in_specs=(P(ctx, "head"), P(ctx, "head"), P(ctx, "head"), P("head", None, None)),
        out_specs=(P(ctx, "head"), P(ctx, None), P(None, "head")),
        check_vma=False,
    )
```

```python
import functools
import math

import jax
import jax.numpy as jnp
from jax import lax
from jax.experimental import pallas as pl
from jax.experimental.pallas import tpu as pltpu
from jax.sharding import PartitionSpec as P

HD = 128
GQ = 8
TILE = 128
PIVOTS = 20
NEAR = 4
FAR = 4
PANEL = 40
STRIP = 8
PIECE = 16
UNIT = 16
SLOTS = 7
NEG = -1e30
ROPE_BASE = 500000.0
VMEM_LIMIT = 48 * 1024 * 1024


def angles(positions, width):
    inverse = jnp.exp(
        -math.log(ROPE_BASE) * 2.0 * jnp.arange(width // 2, dtype=jnp.float32) / width
    )
    turning = positions[:, None] * inverse[None, :]
    cosine, sine = jnp.cos(turning), jnp.sin(turning)
    return (
        jnp.concatenate([cosine, cosine], axis=1),
        jnp.concatenate([-sine, sine], axis=1),
    )


def turn(head_vals, cosine, signed_sine):
    return head_vals * cosine + pltpu.roll(head_vals, HD // 2, 1) * signed_sine


def params():
    return pltpu.CompilerParams(vmem_limit_bytes=VMEM_LIMIT)


def iota(shape, dim):
    return lax.broadcasted_iota(jnp.int32, shape, dim)


def pivots_kernel(keys_ref, piv_ref):
    first = (iota((32, HD), 0) == iota((32, HD), 1)).astype(jnp.bfloat16)
    pivots = lax.dot_general(
        first, keys_ref[...], (((1,), (1,)), ((), ())), preferred_element_type=jnp.float32
    ).astype(jnp.bfloat16)
    for head in range(piv_ref.shape[0]):
        piv_ref[head] = pivots


def prepare_kernel(keys_ref, values_ref, cos_ref, sin_ref, kv_ref):
    keys = keys_ref[...].astype(jnp.float32)
    kv_ref[0:TILE, :] = turn(keys, cos_ref[...], sin_ref[...]).astype(jnp.bfloat16)
    kv_ref[TILE:, :] = values_ref[...]


def queries_kernel(me_ref, mask_ref, queries_ref, cos_ref, sin_ref, out_ref, bias_ref):
    cosine, sine = cos_ref[...], sin_ref[...]
    for g in range(GQ):
        lanes = slice(g * HD, (g + 1) * HD)
        query = turn(queries_ref[:, lanes].astype(jnp.float32), cosine, sine)
        out_ref[:, lanes] = query.astype(jnp.bfloat16)
    mask = mask_ref[0]
    count = jnp.sum(jnp.where(iota(mask.shape, 0) == me_ref[0], mask, 0)) - 1
    width = SLOTS * TILE
    slot = iota((TILE, width), 1) % (SLOTS * PIECE) // PIECE
    bias_ref[:, 0:width] = jnp.where(slot < count, 0.0, NEG)
    below = iota((TILE, TILE), 1) <= iota((TILE, TILE), 0)
    bias_ref[:, width:] = jnp.where(below, 0.0, NEG)


def index_kernel(stride, far_ref, mask_ref, out_ref):
    tiles = mask_ref.shape[1]
    dests = out_ref.shape[0]
    mask = mask_ref[0].astype(jnp.bfloat16)
    dest = iota((dests, tiles), 0)
    tile = dest // NEAR * FAR * NEAR + far_ref[0] * NEAR + dest % NEAR
    own = (tile == iota((dests, tiles), 1)).astype(jnp.bfloat16)
    mine = jnp.dot(own, mask, preferred_element_type=jnp.float32)
    mine = mine * (1.0 - own.astype(jnp.float32))
    before = (iota((tiles, tiles), 0) < iota((tiles, tiles), 1)).astype(jnp.bfloat16)
    rank = jnp.dot(mine.astype(jnp.bfloat16), before, preferred_element_type=jnp.float32)
    col = iota((dests, tiles), 1)
    place = col // NEAR % FAR * stride + (col // (FAR * NEAR) * NEAR + col % NEAR) * PIECE
    place = place.astype(jnp.float32) * mine
    lane = iota(out_ref.shape, 1)
    found = jnp.zeros(out_ref.shape, jnp.float32)
    for slot in range(SLOTS):
        value = jnp.sum(jnp.where(rank == slot, place, 0.0), axis=1, keepdims=True)
        found = jnp.where(lane == slot, value, found)
    out_ref[...] = found.astype(jnp.int32)


def two_terms(total):
    high = total.astype(jnp.bfloat16).astype(jnp.float32)
    return jnp.concatenate([high, total - high], axis=0).astype(jnp.bfloat16)


def one_term(terms):
    terms = terms.astype(jnp.float32)
    half = terms.shape[0] // 2
    return terms[0:half] + terms[half:]


def fold(cross, gram, all_ref):
    rank, half = gram.shape[0], 64
    rest = rank - 128
    row, lane = iota((half, 128), 0), iota((half, 128), 1)
    low = gram[half:128, 0:128]
    diagonal = jnp.sum(jnp.where(lane == row + half, low, 0.0), axis=1, keepdims=True)
    corner = jnp.concatenate(
        [gram[128:, 128:], jnp.zeros((rest, 128 - rest), jnp.float32)], axis=1
    )
    hidden = jnp.concatenate(
        [
            corner,
            pltpu.roll(corner, 128 - rest // 2, 1),
            jnp.broadcast_to(diagonal, (half, 128)),
            jnp.zeros((rank - 2 * rest - half, 128), jnp.float32),
        ],
        axis=0,
    )
    all_ref[0:rank, :] = jnp.where(iota((rank, 128), 1) < PIVOTS, hidden, cross)
    keep = (lane < half) & (lane <= row)
    all_ref[rank:rank + half, :] = jnp.where(keep, gram[0:half, 0:128], pltpu.roll(low, half, 1))
    all_ref[rank + half:, :] = gram[128:, 0:128]


def unfold(head, inverse, sums_ref, work_ref):
    rank, half = work_ref.shape[0], 64
    rest = rank - 128
    row, lane = iota((half, 128), 0), iota((half, 128), 1)
    mixed = sums_ref[rank:rank + half, :] * inverse
    turned = pltpu.roll(mixed, half, 1)
    diagonal = jnp.broadcast_to(sums_ref[2 * rest:2 * rest + half, 0:1], (half, 128)) * inverse
    top = jnp.where((lane < half) & (lane <= row), mixed, 0.0)
    low = jnp.where(
        (lane < half) | (lane > row + half), turned, jnp.where(lane == row + half, diagonal, 0.0)
    )
    one_side = jnp.concatenate([top, low], axis=0)
    other = jnp.where(iota((128, 128), 0) == iota((128, 128), 1), 0.0, one_side.T)
    work_ref[0:128, 0:128] = one_side + other
    last = sums_ref[rank + half:, :] * inverse
    work_ref[128:, 0:128] = last
    work_ref[0:128, 128:256] = jnp.concatenate(
        [last, jnp.zeros((128 - rest, 128), jnp.float32)], axis=0
    ).T
    lane = iota((rest, 128), 1)
    second = pltpu.roll(sums_ref[rest:2 * rest, :], rest // 2, 1)
    corner = jnp.where(lane < rest // 2, sums_ref[0:rest, :], second)
    work_ref[128:, 128:256] = jnp.where(lane < rest, corner * inverse, 0.0)
    own = pltpu.roll(work_ref[:, 0:256], 256 - head * PIVOTS, 1)[:, 0:128]
    work_ref[:, 256:384] = jnp.where(
        iota((rank, 128), 1) < PIVOTS, own, sums_ref[0:rank, :] * inverse
    )


def sums_kernel(piv_ref, keys_ref, kv_ref, out_ref, pivt_ref, all_ref):
    heads = piv_ref.shape[0]
    rank = heads * PIVOTS
    padded = piv_ref[...].reshape(heads * 32, TILE)
    line = iota((rank, heads * 32), 0)
    place = line // PIVOTS * 32 + line % PIVOTS
    compact = (place == iota((rank, heads * 32), 1)).astype(jnp.bfloat16)
    pivt = jnp.dot(compact, padded, preferred_element_type=jnp.float32).astype(jnp.bfloat16)
    pivt_ref[...] = pivt
    cross = jnp.dot(pivt, keys_ref[...], preferred_element_type=jnp.float32)
    gram = lax.dot_general(
        pivt, pivt, (((1,), (1,)), ((), ())), preferred_element_type=jnp.float32
    )
    fold(cross, gram, all_ref)
    for dest in range(out_ref.shape[0]):
        out_ref[dest, 0:PIECE] = kv_ref[dest * PIECE:(dest + 1) * PIECE, :]
        out_ref[dest, PIECE:] = two_terms(all_ref[dest * UNIT:(dest + 1) * UNIT, :])


def middle_kernel(in_ref, out_ref):
    near = in_ref.shape[0]
    total = one_term(in_ref[0, PIECE:])
    for source in range(1, near):
        total = total + one_term(in_ref[source, PIECE:])
    terms = two_terms(total)
    for dest in range(out_ref.shape[0]):
        for source in range(near):
            out_ref[dest, source * PIECE:(source + 1) * PIECE] = in_ref[source, 0:PIECE]
        out_ref[dest, near * PIECE:] = terms


def pick_kernel(place_ref, in_ref, out_ref):
    near, stride = out_ref.shape[0], in_ref.shape[0] // FAR
    total = one_term(in_ref[near * PIECE:stride, :])
    for far in range(1, FAR):
        total = total + one_term(in_ref[far * stride + near * PIECE:(far + 1) * stride, :])
    terms = two_terms(total)
    for dest in range(near):
        for slot in range(SLOTS):
            start = pl.multiple_of(place_ref[dest, slot], PIECE)
            out_ref[dest, slot * PIECE:(slot + 1) * PIECE] = in_ref[pl.ds(start, PIECE), :]
        out_ref[dest, SLOTS * PIECE:] = terms


def basis_steps(tokens, head, in_ref, pivt_ref, factor_ref, coeffs_ref, work_ref, sums_ref):
    rank = pivt_ref.shape[0]
    for source in range(in_ref.shape[0]):
        sums_ref[source * UNIT:(source + 1) * UNIT, :] = one_term(in_ref[source, SLOTS * PIECE:])
    unfold(head, 1.0 / tokens, sums_ref, work_ref)
    work_ref[:, 384:512] = pivt_ref[...].astype(jnp.float32)
    gram = work_ref[:, 0:256]
    row, lane = iota(gram.shape, 0), iota(gram.shape, 1)
    diagonal = jnp.where(row == lane, gram, 0.0)
    down = lax.rsqrt(jnp.sum(diagonal, axis=1, keepdims=True))
    along = jnp.sum(diagonal, axis=0, keepdims=True)
    along = lax.rsqrt(jnp.where(lane[0:1, :] < rank, along, 1.0))
    work_ref[:, 0:256] = gram * down * along
    work_ref[:, 256:512] = work_ref[:, 256:512] * down
    for first in range(0, rank, PANEL):
        block = work_ref[first:first + PANEL, :]
        for start in range(first, first + PANEL, STRIP):
            height = block.shape[0]
            columns = [
                jnp.broadcast_to(block[:, at:at + 1], (height, 128))
                for at in range(start, start + STRIP)
            ]
            for step in range(0, STRIP, 2):
                left, right = columns[step], columns[step + 1]
                a, b = left[step:step + 1, :], left[step + 1:step + 2, :]
                c = right[step + 1:step + 2, :]
                root = lax.rsqrt(a)
                second = a * root * lax.rsqrt(a * c - b * b)
                mixed = b * root * root * second
                right = right * second - left * mixed
                left = left * root
                for later in range(step + 2, STRIP):
                    columns[later] = (
                        columns[later] - left * left[later:later + 1, :]
                    ) - right * right[later:later + 1, :]
                root, second, mixed = (jnp.concatenate([v] * 4, axis=1) for v in (root, second, mixed))
                upper, lower = block[step:step + 1, :], block[step + 1:step + 2, :]
                lower = lower * second - upper * mixed
                upper = upper * root
                at = start + step
                work_ref[at:at + 1, :] = upper
                work_ref[at + 1:at + 2, :] = lower
                block = (block - jnp.concatenate([left] * 4, axis=1) * upper) - (
                    jnp.concatenate([right] * 4, axis=1) * lower
                )
                yield
            block = block[STRIP:, :]
        last = first + PANEL
        if last < rank:
            done = work_ref[first:last, :]
            update = lax.dot_general(
                done[:, 0:256], done, (((0,), (0,)), ((), ())),
                precision=lax.Precision.HIGHEST, preferred_element_type=jnp.float32,
            )
            work_ref[last:rank, :] = work_ref[last:rank, :] - update[last:rank, :]
    factor_ref[...] = work_ref[:, 256:384]
    coeffs_ref[...] = work_ref[:, 384:512]


def attend_steps(queries_ref, bias_ref, in_ref, kv_ref, out_ref):
    per_dest = SLOTS * PIECE
    half = in_ref.shape[0] // 2
    width = half * per_dest
    keys = jnp.concatenate(
        [in_ref[0:half, 0:per_dest].reshape(width, HD), kv_ref[0:TILE, :]], axis=0
    )
    values = jnp.concatenate(
        [in_ref[half:, 0:per_dest].reshape(width, HD), kv_ref[TILE:, :]], axis=0
    )
    scale = HD ** (-0.5) * math.log2(math.e)
    for g in range(GQ):
        lanes = slice(g * HD, (g + 1) * HD)
        scores = lax.dot_general(
            queries_ref[:, lanes], keys, (((1,), (1,)), ((), ())),
            preferred_element_type=jnp.float32,
        ) * scale + bias_ref[...]
        yield
        most = jnp.max(scores, axis=1, keepdims=True)
        yield
        weights = jnp.exp2(scores - most)
        totals = jnp.sum(weights, axis=1, keepdims=True)
        yield
        mixed = jnp.dot(
            weights.astype(jnp.bfloat16), values, preferred_element_type=jnp.float32
        )
        yield
        out_ref[:, lanes] = (mixed / totals).astype(jnp.bfloat16)


def finish_kernel(
    tokens, head_ref, queries_ref, bias_ref, in_ref, kv_ref, pivt_ref,
    out_ref, factor_ref, coeffs_ref, work_ref, sums_ref,
):
    basis = basis_steps(
        tokens, head_ref[0], in_ref, pivt_ref, factor_ref, coeffs_ref, work_ref, sums_ref
    )
    attend = attend_steps(queries_ref, bias_ref, in_ref, kv_ref, out_ref)
    steps = pivt_ref.shape[0] // 2
    given = 0
    for step in range(steps):
        next(basis, None)
        while given * steps < step * 4 * GQ:
            next(attend, None)
            given += 1
    for rest in (attend, basis):
        for _ in rest:
            pass


def on_device(queries, keys, values, tile_mask):
    near_axes = ("x", "near")
    near_size = lax.axis_size(near_axes)
    far_size = lax.axis_size("far")
    head_size = lax.axis_size("head")
    far_index = lax.axis_index("far")
    ctx_index = lax.axis_index(("x", "far", "near"))
    tok_rows = keys.shape[0]
    token_total = tok_rows * near_size * far_size
    rank = head_size * PIVOTS
    positions = ctx_index * tok_rows + lax.iota(jnp.int32, tok_rows)
    cosine, sine = angles(positions.astype(jnp.float32), HD)
    shape = jax.ShapeDtypeStruct
    bf16, f32 = jnp.bfloat16, jnp.float32
    smem, vmem = pl.BlockSpec(memory_space=pltpu.SMEM), pl.BlockSpec(memory_space=pltpu.VMEM)

    def call(kernel, name, out_shape, scalars, *arrays, scratch=()):
        return pl.pallas_call(
            kernel,
            out_shape=out_shape,
            in_specs=[smem] * scalars + [vmem] * (len(arrays) - scalars),
            scratch_shapes=scratch,
            compiler_params=params(),
            name=name,
        )(*arrays)

    pivots = call(pivots_kernel, "pivots", shape((head_size, 32, TILE), bf16), 0, keys)
    pivots = lax.all_to_all(pivots, "head", 0, 0)
    kv = call(
        prepare_kernel, "prepare", shape((2 * TILE, HD), bf16), 0, keys, values, cosine, sine
    )
    stride = near_size * PIECE + 2 * UNIT
    places = call(
        functools.partial(index_kernel, stride), "index",
        shape((near_size, 128), jnp.int32), 1, far_index.reshape(1), tile_mask,
    )
    turned, bias = call(
        queries_kernel, "queries",
        (shape(queries.shape, bf16), shape((TILE, (SLOTS + 1) * TILE), f32)), 1,
        ctx_index.reshape(1), tile_mask, queries, cosine, sine,
    )
    pivots, kv, places, turned, bias, head_index = lax.optimization_barrier(
        (pivots, kv, places, turned, bias, lax.axis_index("head").reshape(1))
    )
    first, pivt = call(
        sums_kernel, "sums",
        (shape((near_size, PIECE + 2 * UNIT, HD), bf16), shape((rank, TILE), bf16)), 0,
        pivots, keys, kv,
        scratch=[pltpu.VMEM((near_size * UNIT, HD), f32)],
    )
    first = lax.all_to_all(first, near_axes, 0, 0)
    second = call(middle_kernel, "middle", shape((far_size, stride, HD), bf16), 0, first)
    second = lax.all_to_all(second, "far", 0, 0)
    third = call(
        pick_kernel, "pick", shape((near_size, SLOTS * PIECE + 2 * UNIT, HD), bf16), 1,
        places, second.reshape(far_size * stride, HD),
    )
    third = lax.all_to_all(third, near_axes, 0, 0)

    attn_out, key_factor, coeffs = call(
        functools.partial(finish_kernel, float(token_total)), "finish",
        (shape(queries.shape, bf16), shape((rank, HD), f32), shape((rank, TILE), f32)), 1,
        head_index, turned, bias, third, kv, pivt,
        scratch=[pltpu.VMEM((rank, 512), f32), pltpu.VMEM((near_size * UNIT, HD), f32)],
    )
    return (attn_out, coeffs.T, key_factor)


def solution(mesh):
    ctx_size, head_size = mesh.shape["ctx"], mesh.shape["head"]
    split = jax.sharding.Mesh(
        mesh.devices.reshape(ctx_size // (FAR * NEAR), FAR, NEAR, head_size),
        ("x", "far", "near", "head"),
    )
    ctx = ("x", "far", "near")
    return jax.shard_map(
        on_device,
        mesh=split,
        in_specs=(P(ctx, "head"), P(ctx, "head"), P(ctx, "head"), P("head", None, None)),
        out_specs=(P(ctx, "head"), P(ctx, None), P(None, "head")),
        check_vma=False,
    )
```

```python
import functools
import math

import jax
import jax.numpy as jnp
from jax import lax
from jax.experimental import pallas as pl
from jax.experimental.pallas import tpu as pltpu
from jax.sharding import PartitionSpec as P

HD = 128
GQ = 8
TILE = 128
PIVOTS = 20
NEAR = 4
FAR = 4
PANEL = 40
STRIP = 8
TOGETHER = 2
PIECE = 16
UNIT = 16
SLOTS = 7
NEG = -1e30
ROPE_BASE = 500000.0
VMEM_LIMIT = 48 * 1024 * 1024


def angles(positions, width):
    inverse = jnp.exp(
        -math.log(ROPE_BASE) * 2.0 * jnp.arange(width // 2, dtype=jnp.float32) / width
    )
    turning = positions[:, None] * inverse[None, :]
    cosine, sine = jnp.cos(turning), jnp.sin(turning)
    return (
        jnp.concatenate([cosine, cosine], axis=1),
        jnp.concatenate([-sine, sine], axis=1),
    )


def turn(head_vals, cosine, signed_sine):
    return head_vals * cosine + pltpu.roll(head_vals, HD // 2, 1) * signed_sine


def params():
    return pltpu.CompilerParams(vmem_limit_bytes=VMEM_LIMIT)


def iota(shape, dim):
    return lax.broadcasted_iota(jnp.int32, shape, dim)


def pivots_kernel(keys_ref, piv_ref):
    first = (iota((32, HD), 0) == iota((32, HD), 1)).astype(jnp.bfloat16)
    pivots = lax.dot_general(
        first, keys_ref[...], (((1,), (1,)), ((), ())), preferred_element_type=jnp.float32
    ).astype(jnp.bfloat16)
    for head in range(piv_ref.shape[0]):
        piv_ref[head] = pivots


def prepare_kernel(keys_ref, values_ref, cos_ref, sin_ref, kv_ref):
    keys = keys_ref[...].astype(jnp.float32)
    kv_ref[0:TILE, :] = turn(keys, cos_ref[...], sin_ref[...]).astype(jnp.bfloat16)
    kv_ref[TILE:, :] = values_ref[...]


def queries_kernel(me_ref, mask_ref, queries_ref, cos_ref, sin_ref, out_ref, bias_ref):
    cosine, sine = cos_ref[...], sin_ref[...]
    for g in range(GQ):
        lanes = slice(g * HD, (g + 1) * HD)
        query = turn(queries_ref[:, lanes].astype(jnp.float32), cosine, sine)
        out_ref[g * TILE:(g + 1) * TILE, :] = query.astype(jnp.bfloat16)
    mask = mask_ref[0]
    count = jnp.sum(jnp.where(iota(mask.shape, 0) == me_ref[0], mask, 0)) - 1
    width = SLOTS * TILE
    slot = iota((TILE, width), 1) % (SLOTS * PIECE) // PIECE
    bias_ref[:, 0:width] = jnp.where(slot < count, 0.0, NEG)
    below = iota((TILE, TILE), 1) <= iota((TILE, TILE), 0)
    bias_ref[:, width:] = jnp.where(below, 0.0, NEG)


def index_kernel(stride, far_ref, mask_ref, out_ref):
    tiles = mask_ref.shape[1]
    dests = out_ref.shape[0]
    mask = mask_ref[0].astype(jnp.bfloat16)
    dest = iota((dests, tiles), 0)
    tile = dest // NEAR * FAR * NEAR + far_ref[0] * NEAR + dest % NEAR
    own = (tile == iota((dests, tiles), 1)).astype(jnp.bfloat16)
    mine = jnp.dot(own, mask, preferred_element_type=jnp.float32)
    mine = mine * (1.0 - own.astype(jnp.float32))
    before = (iota((tiles, tiles), 0) < iota((tiles, tiles), 1)).astype(jnp.bfloat16)
    rank = jnp.dot(mine.astype(jnp.bfloat16), before, preferred_element_type=jnp.float32)
    col = iota((dests, tiles), 1)
    place = col // NEAR % FAR * stride + (col // (FAR * NEAR) * NEAR + col % NEAR) * PIECE
    place = place.astype(jnp.float32) * mine
    lane = iota(out_ref.shape, 1)
    found = jnp.zeros(out_ref.shape, jnp.float32)
    for slot in range(SLOTS):
        value = jnp.sum(jnp.where(rank == slot, place, 0.0), axis=1, keepdims=True)
        found = jnp.where(lane == slot, value, found)
    out_ref[...] = found.astype(jnp.int32)


def two_terms(total):
    high = total.astype(jnp.bfloat16).astype(jnp.float32)
    return jnp.concatenate([high, total - high], axis=0).astype(jnp.bfloat16)


def one_term(terms):
    terms = terms.astype(jnp.float32)
    half = terms.shape[0] // 2
    return terms[0:half] + terms[half:]


def fold(cross, gram, all_ref):
    rank, half = gram.shape[0], 64
    rest = rank - 128
    row, lane = iota((half, 128), 0), iota((half, 128), 1)
    low = gram[half:128, 0:128]
    diagonal = jnp.sum(jnp.where(lane == row + half, low, 0.0), axis=1, keepdims=True)
    corner = jnp.concatenate(
        [gram[128:, 128:], jnp.zeros((rest, 128 - rest), jnp.float32)], axis=1
    )
    hidden = jnp.concatenate(
        [
            corner,
            pltpu.roll(corner, 128 - rest // 2, 1),
            jnp.broadcast_to(diagonal, (half, 128)),
            jnp.zeros((rank - 2 * rest - half, 128), jnp.float32),
        ],
        axis=0,
    )
    all_ref[0:rank, :] = jnp.where(iota((rank, 128), 1) < PIVOTS, hidden, cross)
    keep = (lane < half) & (lane <= row)
    all_ref[rank:rank + half, :] = jnp.where(keep, gram[0:half, 0:128], pltpu.roll(low, half, 1))
    all_ref[rank + half:, :] = gram[128:, 0:128]


def unfold(head, inverse, sums_ref, work_ref):
    rank, half = work_ref.shape[0], 64
    rest = rank - 128
    row, lane = iota((half, 128), 0), iota((half, 128), 1)
    mixed = sums_ref[rank:rank + half, :] * inverse
    turned = pltpu.roll(mixed, half, 1)
    diagonal = jnp.broadcast_to(sums_ref[2 * rest:2 * rest + half, 0:1], (half, 128)) * inverse
    top = jnp.where((lane < half) & (lane <= row), mixed, 0.0)
    low = jnp.where(
        (lane < half) | (lane > row + half), turned, jnp.where(lane == row + half, diagonal, 0.0)
    )
    one_side = jnp.concatenate([top, low], axis=0)
    other = jnp.where(iota((128, 128), 0) == iota((128, 128), 1), 0.0, one_side.T)
    work_ref[0:128, 0:128] = one_side + other
    last = sums_ref[rank + half:, :] * inverse
    work_ref[128:, 0:128] = last
    work_ref[0:128, 128:256] = jnp.concatenate(
        [last, jnp.zeros((128 - rest, 128), jnp.float32)], axis=0
    ).T
    lane = iota((rest, 128), 1)
    second = pltpu.roll(sums_ref[rest:2 * rest, :], rest // 2, 1)
    corner = jnp.where(lane < rest // 2, sums_ref[0:rest, :], second)
    work_ref[128:, 128:256] = jnp.where(lane < rest, corner * inverse, 0.0)
    own = pltpu.roll(work_ref[:, 0:256], 256 - head * PIVOTS, 1)[:, 0:128]
    work_ref[:, 256:384] = jnp.where(
        iota((rank, 128), 1) < PIVOTS, own, sums_ref[0:rank, :] * inverse
    )


def sums_kernel(piv_ref, keys_ref, kv_ref, out_ref, pivt_ref, all_ref):
    heads = piv_ref.shape[0]
    rank = heads * PIVOTS
    padded = piv_ref[...].reshape(heads * 32, TILE)
    line = iota((rank, heads * 32), 0)
    place = line // PIVOTS * 32 + line % PIVOTS
    compact = (place == iota((rank, heads * 32), 1)).astype(jnp.bfloat16)
    pivt = jnp.dot(compact, padded, preferred_element_type=jnp.float32).astype(jnp.bfloat16)
    pivt_ref[...] = pivt
    cross = jnp.dot(pivt, keys_ref[...], preferred_element_type=jnp.float32)
    gram = lax.dot_general(
        pivt, pivt, (((1,), (1,)), ((), ())), preferred_element_type=jnp.float32
    )
    fold(cross, gram, all_ref)
    for dest in range(out_ref.shape[0]):
        out_ref[dest, 0:PIECE] = kv_ref[dest * PIECE:(dest + 1) * PIECE, :]
        out_ref[dest, PIECE:] = two_terms(all_ref[dest * UNIT:(dest + 1) * UNIT, :])


def middle_kernel(in_ref, out_ref):
    near = in_ref.shape[0]
    total = one_term(in_ref[0, PIECE:])
    for source in range(1, near):
        total = total + one_term(in_ref[source, PIECE:])
    terms = two_terms(total)
    for dest in range(out_ref.shape[0]):
        for source in range(near):
            out_ref[dest, source * PIECE:(source + 1) * PIECE] = in_ref[source, 0:PIECE]
        out_ref[dest, near * PIECE:] = terms


def pick_kernel(place_ref, in_ref, out_ref):
    near, stride = out_ref.shape[0], in_ref.shape[0] // FAR
    total = one_term(in_ref[near * PIECE:stride, :])
    for far in range(1, FAR):
        total = total + one_term(in_ref[far * stride + near * PIECE:(far + 1) * stride, :])
    terms = two_terms(total)
    for dest in range(near):
        for slot in range(SLOTS):
            start = pl.multiple_of(place_ref[dest, slot], PIECE)
            out_ref[dest, slot * PIECE:(slot + 1) * PIECE] = in_ref[pl.ds(start, PIECE), :]
        out_ref[dest, SLOTS * PIECE:] = terms


def basis_steps(tokens, head, in_ref, pivt_ref, factor_ref, coeffs_ref, work_ref, sums_ref):
    rank = pivt_ref.shape[0]
    for source in range(in_ref.shape[0]):
        sums_ref[source * UNIT:(source + 1) * UNIT, :] = one_term(in_ref[source, SLOTS * PIECE:])
    unfold(head, 1.0 / tokens, sums_ref, work_ref)
    work_ref[:, 384:512] = pivt_ref[...].astype(jnp.float32)
    for first in range(0, rank, PANEL):
        block = work_ref[first:first + PANEL, :]
        for start in range(first, first + PANEL, STRIP):
            height = block.shape[0]
            columns = [
                jnp.broadcast_to(block[:, at:at + 1], (height, 128))
                for at in range(start, start + STRIP)
            ]
            for step in range(STRIP):
                root = lax.rsqrt(columns[step][step:step + 1, :])
                column = columns[step] * root
                for later in range(step + 1, STRIP):
                    columns[later] = columns[later] - column * column[later:later + 1, :]
                line = block[step:step + 1, :] * jnp.concatenate([root] * 4, axis=1)
                work_ref[start + step:start + step + 1, :] = line
                block = block - jnp.concatenate([column] * 4, axis=1) * line
                yield
            block = block[STRIP:, :]
        last = first + PANEL
        if last < rank:
            done = work_ref[first:last, :]
            update = lax.dot_general(
                done[:, 0:rank], done, (((0,), (0,)), ((), ())),
                precision=lax.Precision.HIGHEST, preferred_element_type=jnp.float32,
            )
            work_ref[last:rank, :] = work_ref[last:rank, :] - update[last:rank, :]
    factor_ref[...] = work_ref[:, 256:384]
    coeffs_ref[...] = work_ref[:, 384:512]


def attend_steps(queries_ref, bias_ref, in_ref, kv_ref, out_ref):
    per_dest = SLOTS * PIECE
    half = in_ref.shape[0] // 2
    width = half * per_dest
    keys = jnp.concatenate(
        [in_ref[0:half, 0:per_dest].reshape(width, HD), kv_ref[0:TILE, :]], axis=0
    )
    values = jnp.concatenate(
        [in_ref[half:, 0:per_dest].reshape(width, HD), kv_ref[TILE:, :]], axis=0
    )
    scale = HD ** (-0.5) * math.log2(math.e)
    bias = jnp.concatenate([bias_ref[...]] * TOGETHER, axis=0)
    for first in range(0, GQ, TOGETHER):
        scores = lax.dot_general(
            queries_ref[first * TILE:(first + TOGETHER) * TILE, :], keys,
            (((1,), (1,)), ((), ())), preferred_element_type=jnp.float32,
        ) * scale + bias
        yield
        most = jnp.max(scores, axis=1, keepdims=True)
        yield
        weights = jnp.exp2(scores - most)
        totals = jnp.sum(weights, axis=1, keepdims=True)
        yield
        mixed = jnp.dot(
            weights.astype(jnp.bfloat16), values, preferred_element_type=jnp.float32
        )
        yield
        mixed = (mixed / totals).astype(jnp.bfloat16)
        for g in range(TOGETHER):
            lanes = slice((first + g) * HD, (first + g + 1) * HD)
            out_ref[:, lanes] = mixed[g * TILE:(g + 1) * TILE]


def finish_kernel(
    tokens, head_ref, queries_ref, bias_ref, in_ref, kv_ref, pivt_ref,
    out_ref, factor_ref, coeffs_ref, work_ref, sums_ref,
):
    basis = basis_steps(
        tokens, head_ref[0], in_ref, pivt_ref, factor_ref, coeffs_ref, work_ref, sums_ref
    )
    attend = attend_steps(queries_ref, bias_ref, in_ref, kv_ref, out_ref)
    steps = pivt_ref.shape[0]
    for step in range(steps):
        next(basis, None)
        if step % (steps // (4 * GQ // TOGETHER)) == 0:
            next(attend, None)
    for rest in (attend, basis):
        for _ in rest:
            pass


def on_device(queries, keys, values, tile_mask):
    near_axes = ("x", "near")
    near_size = lax.axis_size(near_axes)
    far_size = lax.axis_size("far")
    head_size = lax.axis_size("head")
    far_index = lax.axis_index("far")
    ctx_index = lax.axis_index(("x", "far", "near"))
    tok_rows = keys.shape[0]
    token_total = tok_rows * near_size * far_size
    rank = head_size * PIVOTS
    positions = ctx_index * tok_rows + lax.iota(jnp.int32, tok_rows)
    cosine, sine = angles(positions.astype(jnp.float32), HD)
    shape = jax.ShapeDtypeStruct
    bf16, f32 = jnp.bfloat16, jnp.float32
    smem, vmem = pl.BlockSpec(memory_space=pltpu.SMEM), pl.BlockSpec(memory_space=pltpu.VMEM)

    def call(kernel, name, out_shape, scalars, *arrays, scratch=()):
        return pl.pallas_call(
            kernel,
            out_shape=out_shape,
            in_specs=[smem] * scalars + [vmem] * (len(arrays) - scalars),
            scratch_shapes=scratch,
            compiler_params=params(),
            name=name,
        )(*arrays)

    pivots = call(pivots_kernel, "pivots", shape((head_size, 32, TILE), bf16), 0, keys)
    pivots = lax.all_to_all(pivots, "head", 0, 0)
    kv = call(
        prepare_kernel, "prepare", shape((2 * TILE, HD), bf16), 0, keys, values, cosine, sine
    )
    stride = near_size * PIECE + 2 * UNIT
    places = call(
        functools.partial(index_kernel, stride), "index",
        shape((near_size, 128), jnp.int32), 1, far_index.reshape(1), tile_mask,
    )
    turned, bias = call(
        queries_kernel, "queries",
        (shape((GQ * TILE, HD), bf16), shape((TILE, (SLOTS + 1) * TILE), f32)), 1,
        ctx_index.reshape(1), tile_mask, queries, cosine, sine,
    )
    pivots, kv, places, turned, bias, head_index = lax.optimization_barrier(
        (pivots, kv, places, turned, bias, lax.axis_index("head").reshape(1))
    )
    first, pivt = call(
        sums_kernel, "sums",
        (shape((near_size, PIECE + 2 * UNIT, HD), bf16), shape((rank, TILE), bf16)), 0,
        pivots, keys, kv,
        scratch=[pltpu.VMEM((near_size * UNIT, HD), f32)],
    )
    first = lax.all_to_all(first, near_axes, 0, 0)
    second = call(middle_kernel, "middle", shape((far_size, stride, HD), bf16), 0, first)
    second = lax.all_to_all(second, "far", 0, 0)
    third = call(
        pick_kernel, "pick", shape((near_size, SLOTS * PIECE + 2 * UNIT, HD), bf16), 1,
        places, second.reshape(far_size * stride, HD),
    )
    third = lax.all_to_all(third, near_axes, 0, 0)

    attn_out, key_factor, coeffs = call(
        functools.partial(finish_kernel, float(token_total)), "finish",
        (shape(queries.shape, bf16), shape((rank, HD), f32), shape((rank, TILE), f32)), 1,
        head_index, turned, bias, third, kv, pivt,
        scratch=[pltpu.VMEM((rank, 512), f32), pltpu.VMEM((near_size * UNIT, HD), f32)],
    )
    return (attn_out, coeffs.T, key_factor)


def solution(mesh):
    ctx_size, head_size = mesh.shape["ctx"], mesh.shape["head"]
    split = jax.sharding.Mesh(
        mesh.devices.reshape(ctx_size // (FAR * NEAR), FAR, NEAR, head_size),
        ("x", "far", "near", "head"),
    )
    ctx = ("x", "far", "near")
    return jax.shard_map(
        on_device,
        mesh=split,
        in_specs=(P(ctx, "head"), P(ctx, "head"), P(ctx, "head"), P("head", None, None)),
        out_specs=(P(ctx, "head"), P(ctx, None), P(None, "head")),
        check_vma=False,
    )
```

```python
import functools
import math

import jax
import jax.numpy as jnp
from jax import lax
from jax.experimental import pallas as pl
from jax.experimental.pallas import tpu as pltpu
from jax.sharding import PartitionSpec as P

HD = 128
GQ = 8
TILE = 128
PIVOTS = 20
NEAR = 4
FAR = 4
PANEL = 40
STRIP = 8
TOGETHER = 2
PIECE = 16
UNIT = 16
SLOTS = 7
NEG = -1e30
ROPE_BASE = 500000.0
VMEM_LIMIT = 48 * 1024 * 1024


def angles(positions, width):
    inverse = jnp.exp(
        -math.log(ROPE_BASE) * 2.0 * jnp.arange(width // 2, dtype=jnp.float32) / width
    )
    turning = positions[:, None] * inverse[None, :]
    cosine, sine = jnp.cos(turning), jnp.sin(turning)
    return (
        jnp.concatenate([cosine, cosine], axis=1),
        jnp.concatenate([-sine, sine], axis=1),
    )


def turn(head_vals, cosine, signed_sine):
    return head_vals * cosine + pltpu.roll(head_vals, HD // 2, 1) * signed_sine


def params():
    return pltpu.CompilerParams(vmem_limit_bytes=VMEM_LIMIT)


def iota(shape, dim):
    return lax.broadcasted_iota(jnp.int32, shape, dim)


def pivots_kernel(keys_ref, piv_ref):
    first = (iota((32, HD), 0) == iota((32, HD), 1)).astype(jnp.bfloat16)
    pivots = lax.dot_general(
        first, keys_ref[...], (((1,), (1,)), ((), ())), preferred_element_type=jnp.float32
    ).astype(jnp.bfloat16)
    for head in range(piv_ref.shape[0]):
        piv_ref[head] = pivots


def prepare_kernel(keys_ref, values_ref, cos_ref, sin_ref, kv_ref):
    keys = keys_ref[...].astype(jnp.float32)
    kv_ref[0:TILE, :] = turn(keys, cos_ref[...], sin_ref[...]).astype(jnp.bfloat16)
    kv_ref[TILE:, :] = values_ref[...]


def queries_kernel(me_ref, mask_ref, queries_ref, cos_ref, sin_ref, out_ref, bias_ref):
    cosine, sine = cos_ref[...], sin_ref[...]
    for g in range(GQ):
        lanes = slice(g * HD, (g + 1) * HD)
        query = turn(queries_ref[:, lanes].astype(jnp.float32), cosine, sine)
        out_ref[g * TILE:(g + 1) * TILE, :] = query.astype(jnp.bfloat16)
    mask = mask_ref[0]
    count = jnp.sum(jnp.where(iota(mask.shape, 0) == me_ref[0], mask, 0)) - 1
    width = SLOTS * TILE
    slot = iota((TILE, width), 1) % (SLOTS * PIECE) // PIECE
    bias_ref[:, 0:width] = jnp.where(slot < count, 0.0, NEG)
    below = iota((TILE, TILE), 1) <= iota((TILE, TILE), 0)
    bias_ref[:, width:] = jnp.where(below, 0.0, NEG)


def index_kernel(stride, far_ref, mask_ref, out_ref):
    tiles = mask_ref.shape[1]
    dests = out_ref.shape[0]
    mask = mask_ref[0].astype(jnp.bfloat16)
    dest = iota((dests, tiles), 0)
    tile = dest // NEAR * FAR * NEAR + far_ref[0] * NEAR + dest % NEAR
    own = (tile == iota((dests, tiles), 1)).astype(jnp.bfloat16)
    mine = jnp.dot(own, mask, preferred_element_type=jnp.float32)
    mine = mine * (1.0 - own.astype(jnp.float32))
    before = (iota((tiles, tiles), 0) < iota((tiles, tiles), 1)).astype(jnp.bfloat16)
    rank = jnp.dot(mine.astype(jnp.bfloat16), before, preferred_element_type=jnp.float32)
    col = iota((dests, tiles), 1)
    place = col // NEAR % FAR * stride + (col // (FAR * NEAR) * NEAR + col % NEAR) * PIECE
    place = place.astype(jnp.float32) * mine
    lane = iota(out_ref.shape, 1)
    found = jnp.zeros(out_ref.shape, jnp.float32)
    for slot in range(SLOTS):
        value = jnp.sum(jnp.where(rank == slot, place, 0.0), axis=1, keepdims=True)
        found = jnp.where(lane == slot, value, found)
    out_ref[...] = found.astype(jnp.int32)


def two_terms(total):
    high = total.astype(jnp.bfloat16).astype(jnp.float32)
    return jnp.concatenate([high, total - high], axis=0).astype(jnp.bfloat16)


def one_term(terms):
    terms = terms.astype(jnp.float32)
    half = terms.shape[0] // 2
    return terms[0:half] + terms[half:]


def fold(cross, gram, all_ref):
    rank, half = gram.shape[0], 64
    rest = rank - 128
    row, lane = iota((half, 128), 0), iota((half, 128), 1)
    low = gram[half:128, 0:128]
    diagonal = jnp.sum(jnp.where(lane == row + half, low, 0.0), axis=1, keepdims=True)
    corner = jnp.concatenate(
        [gram[128:, 128:], jnp.zeros((rest, 128 - rest), jnp.float32)], axis=1
    )
    hidden = jnp.concatenate(
        [
            corner,
            pltpu.roll(corner, 128 - rest // 2, 1),
            jnp.broadcast_to(diagonal, (half, 128)),
            jnp.zeros((rank - 2 * rest - half, 128), jnp.float32),
        ],
        axis=0,
    )
    all_ref[0:rank, :] = jnp.where(iota((rank, 128), 1) < PIVOTS, hidden, cross)
    keep = (lane < half) & (lane <= row)
    all_ref[rank:rank + half, :] = jnp.where(keep, gram[0:half, 0:128], pltpu.roll(low, half, 1))
    all_ref[rank + half:, :] = gram[128:, 0:128]


def unfold(head, inverse, sums_ref, work_ref):
    rank, half = work_ref.shape[0], 64
    rest = rank - 128
    row, lane = iota((half, 128), 0), iota((half, 128), 1)
    mixed = sums_ref[rank:rank + half, :] * inverse
    turned = pltpu.roll(mixed, half, 1)
    diagonal = jnp.broadcast_to(sums_ref[2 * rest:2 * rest + half, 0:1], (half, 128)) * inverse
    top = jnp.where((lane < half) & (lane <= row), mixed, 0.0)
    low = jnp.where(
        (lane < half) | (lane > row + half), turned, jnp.where(lane == row + half, diagonal, 0.0)
    )
    one_side = jnp.concatenate([top, low], axis=0)
    other = jnp.where(iota((128, 128), 0) == iota((128, 128), 1), 0.0, one_side.T)
    work_ref[0:128, 0:128] = one_side + other
    last = sums_ref[rank + half:, :] * inverse
    work_ref[128:, 0:128] = last
    work_ref[0:128, 128:256] = jnp.concatenate(
        [last, jnp.zeros((128 - rest, 128), jnp.float32)], axis=0
    ).T
    lane = iota((rest, 128), 1)
    second = pltpu.roll(sums_ref[rest:2 * rest, :], rest // 2, 1)
    corner = jnp.where(lane < rest // 2, sums_ref[0:rest, :], second)
    work_ref[128:, 128:256] = jnp.where(lane < rest, corner * inverse, 0.0)
    own = pltpu.roll(work_ref[:, 0:256], 256 - head * PIVOTS, 1)[:, 0:128]
    work_ref[:, 256:384] = jnp.where(
        iota((rank, 128), 1) < PIVOTS, own, sums_ref[0:rank, :] * inverse
    )


def twist(far):
    return far // 2 * 2


def sums_piece(index, far, ref):
    return ref.at[pl.ds(pl.multiple_of((index ^ twist(far)) * UNIT, UNIT), UNIT), :]


def sums_kernel(far_ref, piv_ref, keys_ref, kv_ref, out_ref, pivt_ref, all_ref):
    heads = piv_ref.shape[0]
    rank = heads * PIVOTS
    padded = piv_ref[...].reshape(heads * 32, TILE)
    line = iota((rank, heads * 32), 0)
    place = line // PIVOTS * 32 + line % PIVOTS
    compact = (place == iota((rank, heads * 32), 1)).astype(jnp.bfloat16)
    pivt = jnp.dot(compact, padded, preferred_element_type=jnp.float32).astype(jnp.bfloat16)
    pivt_ref[...] = pivt
    cross = jnp.dot(pivt, keys_ref[...], preferred_element_type=jnp.float32)
    gram = lax.dot_general(
        pivt, pivt, (((1,), (1,)), ((), ())), preferred_element_type=jnp.float32
    )
    fold(cross, gram, all_ref)
    for dest in range(out_ref.shape[0]):
        out_ref[dest, 0:PIECE] = kv_ref[dest * PIECE:(dest + 1) * PIECE, :]
        out_ref[dest, PIECE:] = two_terms(sums_piece(dest, far_ref[0], all_ref)[...])


def middle_kernel(in_ref, out_ref):
    near = in_ref.shape[0]
    total = one_term(in_ref[0, PIECE:])
    for source in range(1, near):
        total = total + one_term(in_ref[source, PIECE:])
    terms = two_terms(total)
    for dest in range(out_ref.shape[0]):
        for source in range(near):
            out_ref[dest, source * PIECE:(source + 1) * PIECE] = in_ref[source, 0:PIECE]
        out_ref[dest, near * PIECE:] = terms


def pick_kernel(place_ref, in_ref, out_ref):
    near, stride = out_ref.shape[0], in_ref.shape[0] // FAR
    total = one_term(in_ref[near * PIECE:stride, :])
    for far in range(1, FAR):
        total = total + one_term(in_ref[far * stride + near * PIECE:(far + 1) * stride, :])
    terms = two_terms(total)
    for dest in range(near):
        for slot in range(SLOTS):
            start = pl.multiple_of(place_ref[dest, slot], PIECE)
            out_ref[dest, slot * PIECE:(slot + 1) * PIECE] = in_ref[pl.ds(start, PIECE), :]
        out_ref[dest, SLOTS * PIECE:] = terms


def basis_steps(tokens, far, head, in_ref, pivt_ref, factor_ref, coeffs_ref, work_ref, sums_ref):
    rank = pivt_ref.shape[0]
    for source in range(in_ref.shape[0]):
        sums_piece(source, far, sums_ref)[...] = one_term(in_ref[source, SLOTS * PIECE:])
    unfold(head, 1.0 / tokens, sums_ref, work_ref)
    work_ref[:, 384:512] = pivt_ref[...].astype(jnp.float32)
    for first in range(0, rank, PANEL):
        block = work_ref[first:first + PANEL, :]
        for start in range(first, first + PANEL, STRIP):
            height = block.shape[0]
            columns = [
                jnp.broadcast_to(block[:, at:at + 1], (height, 128))
                for at in range(start, start + STRIP)
            ]
            for step in range(STRIP):
                root = lax.rsqrt(columns[step][step:step + 1, :])
                column = columns[step] * root
                for later in range(step + 1, STRIP):
                    columns[later] = columns[later] - column * column[later:later + 1, :]
                line = block[step:step + 1, :] * jnp.concatenate([root] * 4, axis=1)
                work_ref[start + step:start + step + 1, :] = line
                block = block - jnp.concatenate([column] * 4, axis=1) * line
                yield
            block = block[STRIP:, :]
        last = first + PANEL
        if last < rank:
            done = work_ref[first:last, :]
            update = lax.dot_general(
                done[:, 0:rank], done, (((0,), (0,)), ((), ())),
                precision=lax.Precision.HIGHEST, preferred_element_type=jnp.float32,
            )
            work_ref[last:rank, :] = work_ref[last:rank, :] - update[last:rank, :]
    factor_ref[...] = work_ref[:, 256:384]
    coeffs_ref[...] = work_ref[:, 384:512]


def attend_steps(queries_ref, bias_ref, in_ref, kv_ref, out_ref):
    per_dest = SLOTS * PIECE
    half = in_ref.shape[0] // 2
    width = half * per_dest
    keys = jnp.concatenate(
        [in_ref[0:half, 0:per_dest].reshape(width, HD), kv_ref[0:TILE, :]], axis=0
    )
    values = jnp.concatenate(
        [in_ref[half:, 0:per_dest].reshape(width, HD), kv_ref[TILE:, :]], axis=0
    )
    scale = HD ** (-0.5) * math.log2(math.e)
    bias = jnp.concatenate([bias_ref[...]] * TOGETHER, axis=0)
    for first in range(0, GQ, TOGETHER):
        scores = lax.dot_general(
            queries_ref[first * TILE:(first + TOGETHER) * TILE, :], keys,
            (((1,), (1,)), ((), ())), preferred_element_type=jnp.float32,
        ) * scale + bias
        yield
        most = jnp.max(scores, axis=1, keepdims=True)
        yield
        weights = jnp.exp2(scores - most)
        totals = jnp.sum(weights, axis=1, keepdims=True)
        yield
        mixed = jnp.dot(
            weights.astype(jnp.bfloat16), values, preferred_element_type=jnp.float32
        )
        yield
        mixed = (mixed / totals).astype(jnp.bfloat16)
        for g in range(TOGETHER):
            lanes = slice((first + g) * HD, (first + g + 1) * HD)
            out_ref[:, lanes] = mixed[g * TILE:(g + 1) * TILE]


def finish_kernel(
    tokens, far_ref, head_ref, queries_ref, bias_ref, in_ref, kv_ref, pivt_ref,
    out_ref, factor_ref, coeffs_ref, work_ref, sums_ref,
):
    basis = basis_steps(
        tokens, far_ref[0], head_ref[0], in_ref, pivt_ref,
        factor_ref, coeffs_ref, work_ref, sums_ref,
    )
    attend = attend_steps(queries_ref, bias_ref, in_ref, kv_ref, out_ref)
    steps = pivt_ref.shape[0]
    for step in range(steps):
        next(basis, None)
        if step % (steps // (4 * GQ // TOGETHER)) == 0:
            next(attend, None)
    for rest in (attend, basis):
        for _ in rest:
            pass


def on_device(queries, keys, values, tile_mask):
    near_axes = ("x", "near")
    near_size = lax.axis_size(near_axes)
    far_size = lax.axis_size("far")
    head_size = lax.axis_size("head")
    far_index = lax.axis_index("far")
    ctx_index = lax.axis_index(("x", "far", "near"))
    tok_rows = keys.shape[0]
    token_total = tok_rows * near_size * far_size
    rank = head_size * PIVOTS
    positions = ctx_index * tok_rows + lax.iota(jnp.int32, tok_rows)
    cosine, sine = angles(positions.astype(jnp.float32), HD)
    shape = jax.ShapeDtypeStruct
    bf16, f32 = jnp.bfloat16, jnp.float32
    smem, vmem = pl.BlockSpec(memory_space=pltpu.SMEM), pl.BlockSpec(memory_space=pltpu.VMEM)

    def call(kernel, name, out_shape, scalars, *arrays, scratch=()):
        return pl.pallas_call(
            kernel,
            out_shape=out_shape,
            in_specs=[smem] * scalars + [vmem] * (len(arrays) - scalars),
            scratch_shapes=scratch,
            compiler_params=params(),
            name=name,
        )(*arrays)

    pivots = call(pivots_kernel, "pivots", shape((head_size, 32, TILE), bf16), 0, keys)
    pivots = lax.all_to_all(pivots, "head", 0, 0)
    kv = call(
        prepare_kernel, "prepare", shape((2 * TILE, HD), bf16), 0, keys, values, cosine, sine
    )
    stride = near_size * PIECE + 2 * UNIT
    places = call(
        functools.partial(index_kernel, stride), "index",
        shape((near_size, 128), jnp.int32), 1, far_index.reshape(1), tile_mask,
    )
    turned, bias = call(
        queries_kernel, "queries",
        (shape((GQ * TILE, HD), bf16), shape((TILE, (SLOTS + 1) * TILE), f32)), 1,
        ctx_index.reshape(1), tile_mask, queries, cosine, sine,
    )
    far_index = far_index.reshape(1)
    pivots, kv, places, turned, bias, far_index, head_index = lax.optimization_barrier(
        (pivots, kv, places, turned, bias, far_index, lax.axis_index("head").reshape(1))
    )
    first, pivt = call(
        sums_kernel, "sums",
        (shape((near_size, PIECE + 2 * UNIT, HD), bf16), shape((rank, TILE), bf16)), 1,
        far_index, pivots, keys, kv,
        scratch=[pltpu.VMEM((near_size * UNIT, HD), f32)],
    )
    first = lax.all_to_all(first, near_axes, 0, 0)
    second = call(middle_kernel, "middle", shape((far_size, stride, HD), bf16), 0, first)
    groups = [
        [far * NEAR + (group ^ twist(far)) for far in range(FAR)] for group in range(NEAR)
    ]
    second = lax.all_to_all(second, ("far", "near"), 0, 0, axis_index_groups=groups)
    third = call(
        pick_kernel, "pick", shape((near_size, SLOTS * PIECE + 2 * UNIT, HD), bf16), 1,
        places, second.reshape(far_size * stride, HD),
    )
    third = lax.all_to_all(third, near_axes, 0, 0)

    attn_out, key_factor, coeffs = call(
        functools.partial(finish_kernel, float(token_total)), "finish",
        (shape(queries.shape, bf16), shape((rank, HD), f32), shape((rank, TILE), f32)), 2,
        far_index, head_index, turned, bias, third, kv, pivt,
        scratch=[pltpu.VMEM((rank, 512), f32), pltpu.VMEM((near_size * UNIT, HD), f32)],
    )
    return (attn_out, coeffs.T, key_factor)


def solution(mesh):
    ctx_size, head_size = mesh.shape["ctx"], mesh.shape["head"]
    split = jax.sharding.Mesh(
        mesh.devices.reshape(ctx_size // (FAR * NEAR), FAR, NEAR, head_size),
        ("x", "far", "near", "head"),
    )
    ctx = ("x", "far", "near")
    return jax.shard_map(
        on_device,
        mesh=split,
        in_specs=(P(ctx, "head"), P(ctx, "head"), P(ctx, "head"), P("head", None, None)),
        out_specs=(P(ctx, "head"), P(ctx, None), P(None, "head")),
        check_vma=False,
    )
```

```python
import functools
import math

import jax
import jax.numpy as jnp
from jax import lax
from jax.experimental import pallas as pl
from jax.experimental.pallas import tpu as pltpu
from jax.sharding import PartitionSpec as P

HD = 128
GQ = 8
TILE = 128
PIVOTS = 20
NEAR = 4
FAR = 4
PANEL = 32
STRIP = 8
TOGETHER = 4
PIECE = 16
UNIT = 16
SLOTS = 7
NEG = -1e30
ROPE_BASE = 500000.0
VMEM_LIMIT = 48 * 1024 * 1024


def angles(positions, width):
    inverse = jnp.exp(
        -math.log(ROPE_BASE) * 2.0 * jnp.arange(width // 2, dtype=jnp.float32) / width
    )
    turning = positions[:, None] * inverse[None, :]
    cosine, sine = jnp.cos(turning), jnp.sin(turning)
    return (
        jnp.concatenate([cosine, cosine], axis=1),
        jnp.concatenate([-sine, sine], axis=1),
    )


def turn(head_vals, cosine, signed_sine):
    return head_vals * cosine + pltpu.roll(head_vals, HD // 2, 1) * signed_sine


def params():
    return pltpu.CompilerParams(vmem_limit_bytes=VMEM_LIMIT)


def iota(shape, dim):
    return lax.broadcasted_iota(jnp.int32, shape, dim)


def pivots_kernel(keys_ref, piv_ref):
    first = (iota((32, HD), 0) == iota((32, HD), 1)).astype(jnp.bfloat16)
    pivots = lax.dot_general(
        first, keys_ref[...], (((1,), (1,)), ((), ())), preferred_element_type=jnp.float32
    ).astype(jnp.bfloat16)
    for head in range(piv_ref.shape[0]):
        piv_ref[head] = pivots


def prepare_kernel(keys_ref, values_ref, cos_ref, sin_ref, kv_ref):
    keys = keys_ref[...].astype(jnp.float32)
    kv_ref[0:TILE, :] = turn(keys, cos_ref[...], sin_ref[...]).astype(jnp.bfloat16)
    kv_ref[TILE:, :] = values_ref[...]


def queries_kernel(me_ref, mask_ref, queries_ref, cos_ref, sin_ref, out_ref, bias_ref):
    cosine, sine = cos_ref[...], sin_ref[...]
    for g in range(GQ):
        lanes = slice(g * HD, (g + 1) * HD)
        query = turn(queries_ref[:, lanes].astype(jnp.float32), cosine, sine)
        out_ref[g * TILE:(g + 1) * TILE, :] = query.astype(jnp.bfloat16)
    mask = mask_ref[0]
    count = jnp.sum(jnp.where(iota(mask.shape, 0) == me_ref[0], mask, 0)) - 1
    width = SLOTS * TILE
    slot = iota((TILE, width), 1) % (SLOTS * PIECE) // PIECE
    bias_ref[:, 0:width] = jnp.where(slot < count, 0.0, NEG)
    below = iota((TILE, TILE), 1) <= iota((TILE, TILE), 0)
    bias_ref[:, width:] = jnp.where(below, 0.0, NEG)


def index_kernel(stride, far_ref, mask_ref, out_ref):
    tiles = mask_ref.shape[1]
    dests = out_ref.shape[0]
    mask = mask_ref[0].astype(jnp.bfloat16)
    dest = iota((dests, tiles), 0)
    tile = dest // NEAR * FAR * NEAR + far_ref[0] * NEAR + dest % NEAR
    own = (tile == iota((dests, tiles), 1)).astype(jnp.bfloat16)
    mine = jnp.dot(own, mask, preferred_element_type=jnp.float32)
    mine = mine * (1.0 - own.astype(jnp.float32))
    before = (iota((tiles, tiles), 0) < iota((tiles, tiles), 1)).astype(jnp.bfloat16)
    rank = jnp.dot(mine.astype(jnp.bfloat16), before, preferred_element_type=jnp.float32)
    col = iota((dests, tiles), 1)
    place = col // NEAR % FAR * stride + (col // (FAR * NEAR) * NEAR + col % NEAR) * PIECE
    place = place.astype(jnp.float32) * mine
    lane = iota(out_ref.shape, 1)
    found = jnp.zeros(out_ref.shape, jnp.float32)
    for slot in range(SLOTS):
        value = jnp.sum(jnp.where(rank == slot, place, 0.0), axis=1, keepdims=True)
        found = jnp.where(lane == slot, value, found)
    out_ref[...] = found.astype(jnp.int32)


def two_terms(total):
    high = total.astype(jnp.bfloat16).astype(jnp.float32)
    return jnp.concatenate([high, total - high], axis=0).astype(jnp.bfloat16)


def one_term(terms):
    terms = terms.astype(jnp.float32)
    half = terms.shape[0] // 2
    return terms[0:half] + terms[half:]


def fold(cross, gram, all_ref):
    rank, half = gram.shape[0], 64
    rest = rank - 128
    row, lane = iota((half, 128), 0), iota((half, 128), 1)
    low = gram[half:128, 0:128]
    diagonal = jnp.sum(jnp.where(lane == row + half, low, 0.0), axis=1, keepdims=True)
    corner = jnp.concatenate(
        [gram[128:, 128:], jnp.zeros((rest, 128 - rest), jnp.float32)], axis=1
    )
    hidden = jnp.concatenate(
        [
            corner,
            pltpu.roll(corner, 128 - rest // 2, 1),
            jnp.broadcast_to(diagonal, (half, 128)),
            jnp.zeros((rank - 2 * rest - half, 128), jnp.float32),
        ],
        axis=0,
    )
    all_ref[0:rank, :] = jnp.where(iota((rank, 128), 1) < PIVOTS, hidden, cross)
    keep = (lane < half) & (lane <= row)
    all_ref[rank:rank + half, :] = jnp.where(keep, gram[0:half, 0:128], pltpu.roll(low, half, 1))
    all_ref[rank + half:, :] = gram[128:, 0:128]


def unfold(head, inverse, sums_ref, work_ref):
    rank, half = work_ref.shape[0], 64
    rest = rank - 128
    row, lane = iota((half, 128), 0), iota((half, 128), 1)
    mixed = sums_ref[rank:rank + half, :] * inverse
    turned = pltpu.roll(mixed, half, 1)
    diagonal = jnp.broadcast_to(sums_ref[2 * rest:2 * rest + half, 0:1], (half, 128)) * inverse
    top = jnp.where((lane < half) & (lane <= row), mixed, 0.0)
    low = jnp.where(
        (lane < half) | (lane > row + half), turned, jnp.where(lane == row + half, diagonal, 0.0)
    )
    one_side = jnp.concatenate([top, low], axis=0)
    other = jnp.where(iota((128, 128), 0) == iota((128, 128), 1), 0.0, one_side.T)
    work_ref[0:128, 0:128] = one_side + other
    last = sums_ref[rank + half:, :] * inverse
    work_ref[128:, 0:128] = last
    work_ref[0:128, 128:256] = jnp.concatenate(
        [last, jnp.zeros((128 - rest, 128), jnp.float32)], axis=0
    ).T
    lane = iota((rest, 128), 1)
    second = pltpu.roll(sums_ref[rest:2 * rest, :], rest // 2, 1)
    corner = jnp.where(lane < rest // 2, sums_ref[0:rest, :], second)
    work_ref[128:, 128:256] = jnp.where(lane < rest, corner * inverse, 0.0)
    own = pltpu.roll(work_ref[:, 0:256], 256 - head * PIVOTS, 1)[:, 0:128]
    work_ref[:, 256:384] = jnp.where(
        iota((rank, 128), 1) < PIVOTS, own, sums_ref[0:rank, :] * inverse
    )


def twist(far):
    return far // 2 * 2


def sums_piece(index, far, ref):
    return ref.at[pl.ds(pl.multiple_of((index ^ twist(far)) * UNIT, UNIT), UNIT), :]


def sums_kernel(far_ref, piv_ref, keys_ref, kv_ref, out_ref, pivt_ref, all_ref):
    heads = piv_ref.shape[0]
    rank = heads * PIVOTS
    padded = piv_ref[...].reshape(heads * 32, TILE)
    line = iota((rank, heads * 32), 0)
    place = line // PIVOTS * 32 + line % PIVOTS
    compact = (place == iota((rank, heads * 32), 1)).astype(jnp.bfloat16)
    pivt = jnp.dot(compact, padded, preferred_element_type=jnp.float32).astype(jnp.bfloat16)
    pivt_ref[...] = pivt
    cross = jnp.dot(pivt, keys_ref[...], preferred_element_type=jnp.float32)
    gram = lax.dot_general(
        pivt, pivt, (((1,), (1,)), ((), ())), preferred_element_type=jnp.float32
    )
    fold(cross, gram, all_ref)
    for dest in range(out_ref.shape[0]):
        out_ref[dest, 0:PIECE] = kv_ref[dest * PIECE:(dest + 1) * PIECE, :]
        out_ref[dest, PIECE:] = two_terms(sums_piece(dest, far_ref[0], all_ref)[...])


def middle_kernel(in_ref, out_ref):
    near = in_ref.shape[0]
    total = one_term(in_ref[0, PIECE:])
    for source in range(1, near):
        total = total + one_term(in_ref[source, PIECE:])
    terms = two_terms(total)
    for dest in range(out_ref.shape[0]):
        for source in range(near):
            out_ref[dest, source * PIECE:(source + 1) * PIECE] = in_ref[source, 0:PIECE]
        out_ref[dest, near * PIECE:] = terms


def pick_kernel(place_ref, in_ref, out_ref):
    near, stride = out_ref.shape[0], in_ref.shape[0] // FAR
    total = one_term(in_ref[near * PIECE:stride, :])
    for far in range(1, FAR):
        total = total + one_term(in_ref[far * stride + near * PIECE:(far + 1) * stride, :])
    terms = two_terms(total)
    for dest in range(near):
        for slot in range(SLOTS):
            start = pl.multiple_of(place_ref[dest, slot], PIECE)
            out_ref[dest, slot * PIECE:(slot + 1) * PIECE] = in_ref[pl.ds(start, PIECE), :]
        out_ref[dest, SLOTS * PIECE:] = terms


def basis_steps(tokens, far, head, in_ref, pivt_ref, factor_ref, coeffs_ref, work_ref, sums_ref):
    rank = pivt_ref.shape[0]
    for source in range(in_ref.shape[0]):
        sums_piece(source, far, sums_ref)[...] = one_term(in_ref[source, SLOTS * PIECE:])
    unfold(head, 1.0 / tokens, sums_ref, work_ref)
    work_ref[:, 384:512] = pivt_ref[...].astype(jnp.float32)
    for first in range(0, rank, PANEL):
        block = work_ref[first:first + PANEL, :]
        for start in range(first, first + PANEL, STRIP):
            height = block.shape[0]
            columns = [
                jnp.broadcast_to(block[:, at:at + 1], (height, 128))
                for at in range(start, start + STRIP)
            ]
            for step in range(STRIP):
                root = lax.rsqrt(columns[step][step:step + 1, :])
                column = columns[step] * root
                for later in range(step + 1, STRIP):
                    columns[later] = columns[later] - column * column[later:later + 1, :]
                line = block[step:step + 1, :] * jnp.concatenate([root] * 4, axis=1)
                work_ref[start + step:start + step + 1, :] = line
                block = block - jnp.concatenate([column] * 4, axis=1) * line
                yield
            block = block[STRIP:, :]
        last = first + PANEL
        if last < rank:
            done = work_ref[first:last, :]
            update = lax.dot_general(
                done[:, 0:rank], done, (((0,), (0,)), ((), ())),
                precision=lax.Precision.HIGHEST, preferred_element_type=jnp.float32,
            )
            work_ref[last:rank, :] = work_ref[last:rank, :] - update[last:rank, :]
    factor_ref[...] = work_ref[:, 256:384]
    coeffs_ref[...] = work_ref[:, 384:512]


def attend_steps(queries_ref, bias_ref, in_ref, kv_ref, out_ref):
    per_dest = SLOTS * PIECE
    half = in_ref.shape[0] // 2
    width = half * per_dest
    keys = jnp.concatenate(
        [in_ref[0:half, 0:per_dest].reshape(width, HD), kv_ref[0:TILE, :]], axis=0
    )
    values = jnp.concatenate(
        [in_ref[half:, 0:per_dest].reshape(width, HD), kv_ref[TILE:, :]], axis=0
    )
    scale = HD ** (-0.5) * math.log2(math.e)
    bias = jnp.concatenate([bias_ref[...]] * TOGETHER, axis=0)
    for first in range(0, GQ, TOGETHER):
        scores = lax.dot_general(
            queries_ref[first * TILE:(first + TOGETHER) * TILE, :], keys,
            (((1,), (1,)), ((), ())), preferred_element_type=jnp.float32,
        ) * scale + bias
        yield
        most = jnp.max(scores, axis=1, keepdims=True)
        yield
        weights = jnp.exp2(scores - most)
        totals = jnp.sum(weights, axis=1, keepdims=True)
        yield
        mixed = jnp.dot(
            weights.astype(jnp.bfloat16), values, preferred_element_type=jnp.float32
        )
        yield
        mixed = (mixed / totals).astype(jnp.bfloat16)
        for g in range(TOGETHER):
            lanes = slice((first + g) * HD, (first + g + 1) * HD)
            out_ref[:, lanes] = mixed[g * TILE:(g + 1) * TILE]


def finish_kernel(
    tokens, far_ref, head_ref, queries_ref, bias_ref, in_ref, kv_ref, pivt_ref,
    out_ref, factor_ref, coeffs_ref, work_ref, sums_ref,
):
    basis = basis_steps(
        tokens, far_ref[0], head_ref[0], in_ref, pivt_ref,
        factor_ref, coeffs_ref, work_ref, sums_ref,
    )
    attend = attend_steps(queries_ref, bias_ref, in_ref, kv_ref, out_ref)
    steps = pivt_ref.shape[0]
    for step in range(steps):
        next(basis, None)
        if step % (steps // (4 * GQ // TOGETHER)) == 0:
            next(attend, None)
    for rest in (attend, basis):
        for _ in rest:
            pass


def on_device(queries, keys, values, tile_mask):
    near_axes = ("x", "near")
    near_size = lax.axis_size(near_axes)
    far_size = lax.axis_size("far")
    head_size = lax.axis_size("head")
    far_index = lax.axis_index("far")
    ctx_index = lax.axis_index(("x", "far", "near"))
    tok_rows = keys.shape[0]
    token_total = tok_rows * near_size * far_size
    rank = head_size * PIVOTS
    positions = ctx_index * tok_rows + lax.iota(jnp.int32, tok_rows)
    cosine, sine = angles(positions.astype(jnp.float32), HD)
    shape = jax.ShapeDtypeStruct
    bf16, f32 = jnp.bfloat16, jnp.float32
    smem, vmem = pl.BlockSpec(memory_space=pltpu.SMEM), pl.BlockSpec(memory_space=pltpu.VMEM)

    def call(kernel, name, out_shape, scalars, *arrays, scratch=()):
        return pl.pallas_call(
            kernel,
            out_shape=out_shape,
            in_specs=[smem] * scalars + [vmem] * (len(arrays) - scalars),
            scratch_shapes=scratch,
            compiler_params=params(),
            name=name,
        )(*arrays)

    pivots = call(pivots_kernel, "pivots", shape((head_size, 32, TILE), bf16), 0, keys)
    pivots = lax.all_to_all(pivots, "head", 0, 0)
    kv = call(
        prepare_kernel, "prepare", shape((2 * TILE, HD), bf16), 0, keys, values, cosine, sine
    )
    stride = near_size * PIECE + 2 * UNIT
    places = call(
        functools.partial(index_kernel, stride), "index",
        shape((near_size, 128), jnp.int32), 1, far_index.reshape(1), tile_mask,
    )
    turned, bias = call(
        queries_kernel, "queries",
        (shape((GQ * TILE, HD), bf16), shape((TILE, (SLOTS + 1) * TILE), f32)), 1,
        ctx_index.reshape(1), tile_mask, queries, cosine, sine,
    )
    far_index = far_index.reshape(1)
    pivots, kv, places, turned, bias, far_index, head_index = lax.optimization_barrier(
        (pivots, kv, places, turned, bias, far_index, lax.axis_index("head").reshape(1))
    )
    first, pivt = call(
        sums_kernel, "sums",
        (shape((near_size, PIECE + 2 * UNIT, HD), bf16), shape((rank, TILE), bf16)), 1,
        far_index, pivots, keys, kv,
        scratch=[pltpu.VMEM((near_size * UNIT, HD), f32)],
    )
    first = lax.all_to_all(first, near_axes, 0, 0)
    second = call(middle_kernel, "middle", shape((far_size, stride, HD), bf16), 0, first)
    groups = [
        [far * NEAR + (group ^ twist(far)) for far in range(FAR)] for group in range(NEAR)
    ]
    second = lax.all_to_all(second, ("far", "near"), 0, 0, axis_index_groups=groups)
    third = call(
        pick_kernel, "pick", shape((near_size, SLOTS * PIECE + 2 * UNIT, HD), bf16), 1,
        places, second.reshape(far_size * stride, HD),
    )
    third = lax.all_to_all(third, near_axes, 0, 0)

    attn_out, key_factor, coeffs = call(
        functools.partial(finish_kernel, float(token_total)), "finish",
        (shape(queries.shape, bf16), shape((rank, HD), f32), shape((rank, TILE), f32)), 2,
        far_index, head_index, turned, bias, third, kv, pivt,
        scratch=[pltpu.VMEM((rank, 512), f32), pltpu.VMEM((near_size * UNIT, HD), f32)],
    )
    return (attn_out, coeffs.T, key_factor)


def solution(mesh):
    ctx_size, head_size = mesh.shape["ctx"], mesh.shape["head"]
    split = jax.sharding.Mesh(
        mesh.devices.reshape(ctx_size // (FAR * NEAR), FAR, NEAR, head_size),
        ("x", "far", "near", "head"),
    )
    ctx = ("x", "far", "near")
    return jax.shard_map(
        on_device,
        mesh=split,
        in_specs=(P(ctx, "head"), P(ctx, "head"), P(ctx, "head"), P("head", None, None)),
        out_specs=(P(ctx, "head"), P(ctx, None), P(None, "head")),
        check_vma=False,
    )
```

```python
import functools
import math

import jax
import jax.numpy as jnp
from jax import lax
from jax.experimental import pallas as pl
from jax.experimental.pallas import tpu as pltpu
from jax.sharding import PartitionSpec as P

HD = 128
GQ = 8
TILE = 128
PIVOTS = 20
NEAR = 4
FAR = 4
PANEL = 80
STRIP = 8
TOGETHER = 2
PIECE = 16
UNIT = 16
SLOTS = 7
NEG = -1e30
ROPE_BASE = 500000.0
VMEM_LIMIT = 48 * 1024 * 1024


def angles(positions, width):
    inverse = jnp.exp(
        -math.log(ROPE_BASE) * 2.0 * jnp.arange(width // 2, dtype=jnp.float32) / width
    )
    turning = positions[:, None] * inverse[None, :]
    cosine, sine = jnp.cos(turning), jnp.sin(turning)
    return (
        jnp.concatenate([cosine, cosine], axis=1),
        jnp.concatenate([-sine, sine], axis=1),
    )


def turn(head_vals, cosine, signed_sine):
    return head_vals * cosine + pltpu.roll(head_vals, HD // 2, 1) * signed_sine


def params():
    return pltpu.CompilerParams(vmem_limit_bytes=VMEM_LIMIT)


def iota(shape, dim):
    return lax.broadcasted_iota(jnp.int32, shape, dim)


def pivots_kernel(keys_ref, piv_ref):
    first = (iota((32, HD), 0) == iota((32, HD), 1)).astype(jnp.bfloat16)
    pivots = lax.dot_general(
        first, keys_ref[...], (((1,), (1,)), ((), ())), preferred_element_type=jnp.float32
    ).astype(jnp.bfloat16)
    for head in range(piv_ref.shape[0]):
        piv_ref[head] = pivots


def prepare_kernel(keys_ref, values_ref, cos_ref, sin_ref, kv_ref):
    keys = keys_ref[...].astype(jnp.float32)
    kv_ref[0:TILE, :] = turn(keys, cos_ref[...], sin_ref[...]).astype(jnp.bfloat16)
    kv_ref[TILE:, :] = values_ref[...]


def queries_kernel(me_ref, mask_ref, queries_ref, cos_ref, sin_ref, out_ref, bias_ref):
    cosine, sine = cos_ref[...], sin_ref[...]
    for g in range(GQ):
        lanes = slice(g * HD, (g + 1) * HD)
        query = turn(queries_ref[:, lanes].astype(jnp.float32), cosine, sine)
        out_ref[g * TILE:(g + 1) * TILE, :] = query.astype(jnp.bfloat16)
    mask = mask_ref[0]
    count = jnp.sum(jnp.where(iota(mask.shape, 0) == me_ref[0], mask, 0)) - 1
    width = SLOTS * TILE
    slot = iota((TILE, width), 1) % (SLOTS * PIECE) // PIECE
    bias_ref[:, 0:width] = jnp.where(slot < count, 0.0, NEG)
    below = iota((TILE, TILE), 1) <= iota((TILE, TILE), 0)
    bias_ref[:, width:] = jnp.where(below, 0.0, NEG)


def index_kernel(stride, far_ref, mask_ref, out_ref):
    tiles = mask_ref.shape[1]
    dests = out_ref.shape[0]
    mask = mask_ref[0].astype(jnp.bfloat16)
    dest = iota((dests, tiles), 0)
    tile = dest // NEAR * FAR * NEAR + far_ref[0] * NEAR + dest % NEAR
    own = (tile == iota((dests, tiles), 1)).astype(jnp.bfloat16)
    mine = jnp.dot(own, mask, preferred_element_type=jnp.float32)
    mine = mine * (1.0 - own.astype(jnp.float32))
    before = (iota((tiles, tiles), 0) < iota((tiles, tiles), 1)).astype(jnp.bfloat16)
    rank = jnp.dot(mine.astype(jnp.bfloat16), before, preferred_element_type=jnp.float32)
    col = iota((dests, tiles), 1)
    place = col // NEAR % FAR * stride + (col // (FAR * NEAR) * NEAR + col % NEAR) * PIECE
    place = place.astype(jnp.float32) * mine
    lane = iota(out_ref.shape, 1)
    found = jnp.zeros(out_ref.shape, jnp.float32)
    for slot in range(SLOTS):
        value = jnp.sum(jnp.where(rank == slot, place, 0.0), axis=1, keepdims=True)
        found = jnp.where(lane == slot, value, found)
    out_ref[...] = found.astype(jnp.int32)


def two_terms(total):
    high = total.astype(jnp.bfloat16).astype(jnp.float32)
    return jnp.concatenate([high, total - high], axis=0).astype(jnp.bfloat16)


def one_term(terms):
    terms = terms.astype(jnp.float32)
    half = terms.shape[0] // 2
    return terms[0:half] + terms[half:]


def fold(cross, gram, all_ref):
    rank, half = gram.shape[0], 64
    rest = rank - 128
    row, lane = iota((half, 128), 0), iota((half, 128), 1)
    low = gram[half:128, 0:128]
    diagonal = jnp.sum(jnp.where(lane == row + half, low, 0.0), axis=1, keepdims=True)
    corner = jnp.concatenate(
        [gram[128:, 128:], jnp.zeros((rest, 128 - rest), jnp.float32)], axis=1
    )
    hidden = jnp.concatenate(
        [
            corner,
            pltpu.roll(corner, 128 - rest // 2, 1),
            jnp.broadcast_to(diagonal, (half, 128)),
            jnp.zeros((rank - 2 * rest - half, 128), jnp.float32),
        ],
        axis=0,
    )
    all_ref[0:rank, :] = jnp.where(iota((rank, 128), 1) < PIVOTS, hidden, cross)
    keep = (lane < half) & (lane <= row)
    all_ref[rank:rank + half, :] = jnp.where(keep, gram[0:half, 0:128], pltpu.roll(low, half, 1))
    all_ref[rank + half:, :] = gram[128:, 0:128]


def unfold(head, inverse, sums_ref, work_ref):
    rank, half = work_ref.shape[0], 64
    rest = rank - 128
    row, lane = iota((half, 128), 0), iota((half, 128), 1)
    mixed = sums_ref[rank:rank + half, :] * inverse
    turned = pltpu.roll(mixed, half, 1)
    diagonal = jnp.broadcast_to(sums_ref[2 * rest:2 * rest + half, 0:1], (half, 128)) * inverse
    top = jnp.where((lane < half) & (lane <= row), mixed, 0.0)
    low = jnp.where(
        (lane < half) | (lane > row + half), turned, jnp.where(lane == row + half, diagonal, 0.0)
    )
    one_side = jnp.concatenate([top, low], axis=0)
    other = jnp.where(iota((128, 128), 0) == iota((128, 128), 1), 0.0, one_side.T)
    work_ref[0:128, 0:128] = one_side + other
    last = sums_ref[rank + half:, :] * inverse
    work_ref[128:, 0:128] = last
    work_ref[0:128, 128:256] = jnp.concatenate(
        [last, jnp.zeros((128 - rest, 128), jnp.float32)], axis=0
    ).T
    lane = iota((rest, 128), 1)
    second = pltpu.roll(sums_ref[rest:2 * rest, :], rest // 2, 1)
    corner = jnp.where(lane < rest // 2, sums_ref[0:rest, :], second)
    work_ref[128:, 128:256] = jnp.where(lane < rest, corner * inverse, 0.0)
    own = pltpu.roll(work_ref[:, 0:256], 256 - head * PIVOTS, 1)[:, 0:128]
    work_ref[:, 256:384] = jnp.where(
        iota((rank, 128), 1) < PIVOTS, own, sums_ref[0:rank, :] * inverse
    )


def twist(far):
    return far // 2 * 2


def sums_piece(index, far, ref):
    return ref.at[pl.ds(pl.multiple_of((index ^ twist(far)) * UNIT, UNIT), UNIT), :]


def sums_kernel(far_ref, piv_ref, keys_ref, kv_ref, out_ref, pivt_ref, all_ref):
    heads = piv_ref.shape[0]
    rank = heads * PIVOTS
    padded = piv_ref[...].reshape(heads * 32, TILE)
    line = iota((rank, heads * 32), 0)
    place = line // PIVOTS * 32 + line % PIVOTS
    compact = (place == iota((rank, heads * 32), 1)).astype(jnp.bfloat16)
    pivt = jnp.dot(compact, padded, preferred_element_type=jnp.float32).astype(jnp.bfloat16)
    pivt_ref[...] = pivt
    cross = jnp.dot(pivt, keys_ref[...], preferred_element_type=jnp.float32)
    gram = lax.dot_general(
        pivt, pivt, (((1,), (1,)), ((), ())), preferred_element_type=jnp.float32
    )
    fold(cross, gram, all_ref)
    for dest in range(out_ref.shape[0]):
        out_ref[dest, 0:PIECE] = kv_ref[dest * PIECE:(dest + 1) * PIECE, :]
        out_ref[dest, PIECE:] = two_terms(sums_piece(dest, far_ref[0], all_ref)[...])


def middle_kernel(in_ref, out_ref):
    near = in_ref.shape[0]
    total = one_term(in_ref[0, PIECE:])
    for source in range(1, near):
        total = total + one_term(in_ref[source, PIECE:])
    terms = two_terms(total)
    for dest in range(out_ref.shape[0]):
        for source in range(near):
            out_ref[dest, source * PIECE:(source + 1) * PIECE] = in_ref[source, 0:PIECE]
        out_ref[dest, near * PIECE:] = terms


def pick_kernel(place_ref, in_ref, out_ref):
    near, stride = out_ref.shape[0], in_ref.shape[0] // FAR
    total = one_term(in_ref[near * PIECE:stride, :])
    for far in range(1, FAR):
        total = total + one_term(in_ref[far * stride + near * PIECE:(far + 1) * stride, :])
    terms = two_terms(total)
    for dest in range(near):
        for slot in range(SLOTS):
            start = pl.multiple_of(place_ref[dest, slot], PIECE)
            out_ref[dest, slot * PIECE:(slot + 1) * PIECE] = in_ref[pl.ds(start, PIECE), :]
        out_ref[dest, SLOTS * PIECE:] = terms


def basis_steps(tokens, far, head, in_ref, pivt_ref, factor_ref, coeffs_ref, work_ref, sums_ref):
    rank = pivt_ref.shape[0]
    for source in range(in_ref.shape[0]):
        sums_piece(source, far, sums_ref)[...] = one_term(in_ref[source, SLOTS * PIECE:])
    unfold(head, 1.0 / tokens, sums_ref, work_ref)
    work_ref[:, 384:512] = pivt_ref[...].astype(jnp.float32)
    for first in range(0, rank, PANEL):
        block = work_ref[first:first + PANEL, :]
        for start in range(first, first + PANEL, STRIP):
            height = block.shape[0]
            columns = [
                jnp.broadcast_to(block[:, at:at + 1], (height, 128))
                for at in range(start, start + STRIP)
            ]
            for step in range(STRIP):
                root = lax.rsqrt(columns[step][step:step + 1, :])
                column = columns[step] * root
                for later in range(step + 1, STRIP):
                    columns[later] = columns[later] - column * column[later:later + 1, :]
                line = block[step:step + 1, :] * jnp.concatenate([root] * 4, axis=1)
                work_ref[start + step:start + step + 1, :] = line
                block = block - jnp.concatenate([column] * 4, axis=1) * line
                yield
            block = block[STRIP:, :]
        last = first + PANEL
        if last < rank:
            done = work_ref[first:last, :]
            update = lax.dot_general(
                done[:, 0:rank], done, (((0,), (0,)), ((), ())),
                precision=lax.Precision.HIGHEST, preferred_element_type=jnp.float32,
            )
            work_ref[last:rank, :] = work_ref[last:rank, :] - update[last:rank, :]
    factor_ref[...] = work_ref[:, 256:384]
    coeffs_ref[...] = work_ref[:, 384:512]


def attend_steps(queries_ref, bias_ref, in_ref, kv_ref, out_ref):
    per_dest = SLOTS * PIECE
    half = in_ref.shape[0] // 2
    width = half * per_dest
    keys = jnp.concatenate(
        [in_ref[0:half, 0:per_dest].reshape(width, HD), kv_ref[0:TILE, :]], axis=0
    )
    values = jnp.concatenate(
        [in_ref[half:, 0:per_dest].reshape(width, HD), kv_ref[TILE:, :]], axis=0
    )
    scale = HD ** (-0.5) * math.log2(math.e)
    bias = jnp.concatenate([bias_ref[...]] * TOGETHER, axis=0)
    for first in range(0, GQ, TOGETHER):
        scores = lax.dot_general(
            queries_ref[first * TILE:(first + TOGETHER) * TILE, :], keys,
            (((1,), (1,)), ((), ())), preferred_element_type=jnp.float32,
        ) * scale + bias
        yield
        most = jnp.max(scores, axis=1, keepdims=True)
        yield
        weights = jnp.exp2(scores - most)
        totals = jnp.sum(weights, axis=1, keepdims=True)
        yield
        mixed = jnp.dot(
            weights.astype(jnp.bfloat16), values, preferred_element_type=jnp.float32
        )
        yield
        mixed = (mixed / totals).astype(jnp.bfloat16)
        for g in range(TOGETHER):
            lanes = slice((first + g) * HD, (first + g + 1) * HD)
            out_ref[:, lanes] = mixed[g * TILE:(g + 1) * TILE]


def finish_kernel(
    tokens, far_ref, head_ref, queries_ref, bias_ref, in_ref, kv_ref, pivt_ref,
    out_ref, factor_ref, coeffs_ref, work_ref, sums_ref,
):
    basis = basis_steps(
        tokens, far_ref[0], head_ref[0], in_ref, pivt_ref,
        factor_ref, coeffs_ref, work_ref, sums_ref,
    )
    attend = attend_steps(queries_ref, bias_ref, in_ref, kv_ref, out_ref)
    steps = pivt_ref.shape[0]
    for step in range(steps):
        next(basis, None)
        if step % (steps // (4 * GQ // TOGETHER)) == 0:
            next(attend, None)
    for rest in (attend, basis):
        for _ in rest:
            pass


def on_device(queries, keys, values, tile_mask):
    near_axes = ("x", "near")
    near_size = lax.axis_size(near_axes)
    far_size = lax.axis_size("far")
    head_size = lax.axis_size("head")
    far_index = lax.axis_index("far")
    ctx_index = lax.axis_index(("x", "far", "near"))
    tok_rows = keys.shape[0]
    token_total = tok_rows * near_size * far_size
    rank = head_size * PIVOTS
    positions = ctx_index * tok_rows + lax.iota(jnp.int32, tok_rows)
    cosine, sine = angles(positions.astype(jnp.float32), HD)
    shape = jax.ShapeDtypeStruct
    bf16, f32 = jnp.bfloat16, jnp.float32
    smem, vmem = pl.BlockSpec(memory_space=pltpu.SMEM), pl.BlockSpec(memory_space=pltpu.VMEM)

    def call(kernel, name, out_shape, scalars, *arrays, scratch=()):
        return pl.pallas_call(
            kernel,
            out_shape=out_shape,
            in_specs=[smem] * scalars + [vmem] * (len(arrays) - scalars),
            scratch_shapes=scratch,
            compiler_params=params(),
            name=name,
        )(*arrays)

    pivots = call(pivots_kernel, "pivots", shape((head_size, 32, TILE), bf16), 0, keys)
    pivots = lax.all_to_all(pivots, "head", 0, 0)
    kv = call(
        prepare_kernel, "prepare", shape((2 * TILE, HD), bf16), 0, keys, values, cosine, sine
    )
    stride = near_size * PIECE + 2 * UNIT
    places = call(
        functools.partial(index_kernel, stride), "index",
        shape((near_size, 128), jnp.int32), 1, far_index.reshape(1), tile_mask,
    )
    turned, bias = call(
        queries_kernel, "queries",
        (shape((GQ * TILE, HD), bf16), shape((TILE, (SLOTS + 1) * TILE), f32)), 1,
        ctx_index.reshape(1), tile_mask, queries, cosine, sine,
    )
    far_index = far_index.reshape(1)
    pivots, kv, places, turned, bias, far_index, head_index = lax.optimization_barrier(
        (pivots, kv, places, turned, bias, far_index, lax.axis_index("head").reshape(1))
    )
    first, pivt = call(
        sums_kernel, "sums",
        (shape((near_size, PIECE + 2 * UNIT, HD), bf16), shape((rank, TILE), bf16)), 1,
        far_index, pivots, keys, kv,
        scratch=[pltpu.VMEM((near_size * UNIT, HD), f32)],
    )
    first = lax.all_to_all(first, near_axes, 0, 0)
    second = call(middle_kernel, "middle", shape((far_size, stride, HD), bf16), 0, first)
    groups = [
        [far * NEAR + (group ^ twist(far)) for far in range(FAR)] for group in range(NEAR)
    ]
    second = lax.all_to_all(second, ("far", "near"), 0, 0, axis_index_groups=groups)
    third = call(
        pick_kernel, "pick", shape((near_size, SLOTS * PIECE + 2 * UNIT, HD), bf16), 1,
        places, second.reshape(far_size * stride, HD),
    )
    third = lax.all_to_all(third, near_axes, 0, 0)

    attn_out, key_factor, coeffs = call(
        functools.partial(finish_kernel, float(token_total)), "finish",
        (shape(queries.shape, bf16), shape((rank, HD), f32), shape((rank, TILE), f32)), 2,
        far_index, head_index, turned, bias, third, kv, pivt,
        scratch=[pltpu.VMEM((rank, 512), f32), pltpu.VMEM((near_size * UNIT, HD), f32)],
    )
    return (attn_out, coeffs.T, key_factor)


def solution(mesh):
    ctx_size, head_size = mesh.shape["ctx"], mesh.shape["head"]
    split = jax.sharding.Mesh(
        mesh.devices.reshape(ctx_size // (FAR * NEAR), FAR, NEAR, head_size),
        ("x", "far", "near", "head"),
    )
    ctx = ("x", "far", "near")
    return jax.shard_map(
        on_device,
        mesh=split,
        in_specs=(P(ctx, "head"), P(ctx, "head"), P(ctx, "head"), P("head", None, None)),
        out_specs=(P(ctx, "head"), P(ctx, None), P(None, "head")),
        check_vma=False,
    )
```

```python
import functools
import math

import jax
import jax.numpy as jnp
from jax import lax
from jax.experimental import pallas as pl
from jax.experimental.pallas import tpu as pltpu
from jax.sharding import PartitionSpec as P

HD = 128
GQ = 8
TILE = 128
PIVOTS = 20
NEAR = 4
FAR = 4
PANEL = 40
STRIP = 8
AHEAD = 5
TOGETHER = 2
PIECE = 16
UNIT = 16
SLOTS = 7
NEG = -1e30
ROPE_BASE = 500000.0
VMEM_LIMIT = 48 * 1024 * 1024


def angles(positions, width):
    inverse = jnp.exp(
        -math.log(ROPE_BASE) * 2.0 * jnp.arange(width // 2, dtype=jnp.float32) / width
    )
    turning = positions[:, None] * inverse[None, :]
    cosine, sine = jnp.cos(turning), jnp.sin(turning)
    return (
        jnp.concatenate([cosine, cosine], axis=1),
        jnp.concatenate([-sine, sine], axis=1),
    )


def turn(head_vals, cosine, signed_sine):
    return head_vals * cosine + pltpu.roll(head_vals, HD // 2, 1) * signed_sine


def params():
    return pltpu.CompilerParams(vmem_limit_bytes=VMEM_LIMIT)


def iota(shape, dim):
    return lax.broadcasted_iota(jnp.int32, shape, dim)


def pivots_kernel(keys_ref, piv_ref):
    first = (iota((32, HD), 0) == iota((32, HD), 1)).astype(jnp.bfloat16)
    pivots = lax.dot_general(
        first, keys_ref[...], (((1,), (1,)), ((), ())), preferred_element_type=jnp.float32
    ).astype(jnp.bfloat16)
    for head in range(piv_ref.shape[0]):
        piv_ref[head] = pivots


def prepare_kernel(keys_ref, values_ref, cos_ref, sin_ref, kv_ref):
    keys = keys_ref[...].astype(jnp.float32)
    kv_ref[0:TILE, :] = turn(keys, cos_ref[...], sin_ref[...]).astype(jnp.bfloat16)
    kv_ref[TILE:, :] = values_ref[...]


def queries_kernel(me_ref, mask_ref, queries_ref, cos_ref, sin_ref, out_ref, bias_ref):
    cosine, sine = cos_ref[...], sin_ref[...]
    for g in range(GQ):
        lanes = slice(g * HD, (g + 1) * HD)
        query = turn(queries_ref[:, lanes].astype(jnp.float32), cosine, sine)
        out_ref[g * TILE:(g + 1) * TILE, :] = query.astype(jnp.bfloat16)
    mask = mask_ref[0]
    count = jnp.sum(jnp.where(iota(mask.shape, 0) == me_ref[0], mask, 0)) - 1
    width = SLOTS * TILE
    slot = iota((TILE, width), 1) % (SLOTS * PIECE) // PIECE
    bias_ref[:, 0:width] = jnp.where(slot < count, 0.0, NEG)
    below = iota((TILE, TILE), 1) <= iota((TILE, TILE), 0)
    bias_ref[:, width:] = jnp.where(below, 0.0, NEG)


def index_kernel(stride, far_ref, mask_ref, out_ref):
    tiles = mask_ref.shape[1]
    dests = out_ref.shape[0]
    mask = mask_ref[0].astype(jnp.bfloat16)
    dest = iota((dests, tiles), 0)
    tile = dest // NEAR * FAR * NEAR + far_ref[0] * NEAR + dest % NEAR
    own = (tile == iota((dests, tiles), 1)).astype(jnp.bfloat16)
    mine = jnp.dot(own, mask, preferred_element_type=jnp.float32)
    mine = mine * (1.0 - own.astype(jnp.float32))
    before = (iota((tiles, tiles), 0) < iota((tiles, tiles), 1)).astype(jnp.bfloat16)
    rank = jnp.dot(mine.astype(jnp.bfloat16), before, preferred_element_type=jnp.float32)
    col = iota((dests, tiles), 1)
    place = col // NEAR % FAR * stride + (col // (FAR * NEAR) * NEAR + col % NEAR) * PIECE
    place = place.astype(jnp.float32) * mine
    lane = iota(out_ref.shape, 1)
    found = jnp.zeros(out_ref.shape, jnp.float32)
    for slot in range(SLOTS):
        value = jnp.sum(jnp.where(rank == slot, place, 0.0), axis=1, keepdims=True)
        found = jnp.where(lane == slot, value, found)
    out_ref[...] = found.astype(jnp.int32)


def two_terms(total):
    high = total.astype(jnp.bfloat16).astype(jnp.float32)
    return jnp.concatenate([high, total - high], axis=0).astype(jnp.bfloat16)


def one_term(terms):
    terms = terms.astype(jnp.float32)
    half = terms.shape[0] // 2
    return terms[0:half] + terms[half:]


def fold(cross, gram, all_ref):
    rank, half = gram.shape[0], 64
    rest = rank - 128
    row, lane = iota((half, 128), 0), iota((half, 128), 1)
    low = gram[half:128, 0:128]
    diagonal = jnp.sum(jnp.where(lane == row + half, low, 0.0), axis=1, keepdims=True)
    corner = jnp.concatenate(
        [gram[128:, 128:], jnp.zeros((rest, 128 - rest), jnp.float32)], axis=1
    )
    hidden = jnp.concatenate(
        [
            corner,
            pltpu.roll(corner, 128 - rest // 2, 1),
            jnp.broadcast_to(diagonal, (half, 128)),
            jnp.zeros((rank - 2 * rest - half, 128), jnp.float32),
        ],
        axis=0,
    )
    all_ref[0:rank, :] = jnp.where(iota((rank, 128), 1) < PIVOTS, hidden, cross)
    keep = (lane < half) & (lane <= row)
    all_ref[rank:rank + half, :] = jnp.where(keep, gram[0:half, 0:128], pltpu.roll(low, half, 1))
    all_ref[rank + half:, :] = gram[128:, 0:128]


def unfold(head, inverse, sums_ref, work_ref):
    rank, half = work_ref.shape[0], 64
    rest = rank - 128
    row, lane = iota((half, 128), 0), iota((half, 128), 1)
    mixed = sums_ref[rank:rank + half, :] * inverse
    turned = pltpu.roll(mixed, half, 1)
    diagonal = jnp.broadcast_to(sums_ref[2 * rest:2 * rest + half, 0:1], (half, 128)) * inverse
    top = jnp.where((lane < half) & (lane <= row), mixed, 0.0)
    low = jnp.where(
        (lane < half) | (lane > row + half), turned, jnp.where(lane == row + half, diagonal, 0.0)
    )
    one_side = jnp.concatenate([top, low], axis=0)
    other = jnp.where(iota((128, 128), 0) == iota((128, 128), 1), 0.0, one_side.T)
    work_ref[0:128, 0:128] = one_side + other
    last = sums_ref[rank + half:, :] * inverse
    work_ref[128:, 0:128] = last
    work_ref[0:128, 128:256] = jnp.concatenate(
        [last, jnp.zeros((128 - rest, 128), jnp.float32)], axis=0
    ).T
    lane = iota((rest, 128), 1)
    second = pltpu.roll(sums_ref[rest:2 * rest, :], rest // 2, 1)
    corner = jnp.where(lane < rest // 2, sums_ref[0:rest, :], second)
    work_ref[128:, 128:256] = jnp.where(lane < rest, corner * inverse, 0.0)
    own = pltpu.roll(work_ref[:, 0:256], 256 - head * PIVOTS, 1)[:, 0:128]
    work_ref[:, 256:384] = jnp.where(
        iota((rank, 128), 1) < PIVOTS, own, sums_ref[0:rank, :] * inverse
    )


def twist(far):
    return far // 2 * 2


def sums_piece(index, far, ref):
    return ref.at[pl.ds(pl.multiple_of((index ^ twist(far)) * UNIT, UNIT), UNIT), :]


def sums_kernel(far_ref, piv_ref, keys_ref, kv_ref, out_ref, pivt_ref, all_ref):
    heads = piv_ref.shape[0]
    rank = heads * PIVOTS
    padded = piv_ref[...].reshape(heads * 32, TILE)
    line = iota((rank, heads * 32), 0)
    place = line // PIVOTS * 32 + line % PIVOTS
    compact = (place == iota((rank, heads * 32), 1)).astype(jnp.bfloat16)
    pivt = jnp.dot(compact, padded, preferred_element_type=jnp.float32).astype(jnp.bfloat16)
    pivt_ref[...] = pivt
    cross = jnp.dot(pivt, keys_ref[...], preferred_element_type=jnp.float32)
    gram = lax.dot_general(
        pivt, pivt, (((1,), (1,)), ((), ())), preferred_element_type=jnp.float32
    )
    fold(cross, gram, all_ref)
    for dest in range(out_ref.shape[0]):
        out_ref[dest, 0:PIECE] = kv_ref[dest * PIECE:(dest + 1) * PIECE, :]
        out_ref[dest, PIECE:] = two_terms(sums_piece(dest, far_ref[0], all_ref)[...])


def middle_kernel(in_ref, out_ref):
    near = in_ref.shape[0]
    total = one_term(in_ref[0, PIECE:])
    for source in range(1, near):
        total = total + one_term(in_ref[source, PIECE:])
    terms = two_terms(total)
    for dest in range(out_ref.shape[0]):
        for source in range(near):
            out_ref[dest, source * PIECE:(source + 1) * PIECE] = in_ref[source, 0:PIECE]
        out_ref[dest, near * PIECE:] = terms


def pick_kernel(place_ref, in_ref, out_ref):
    near, stride = out_ref.shape[0], in_ref.shape[0] // FAR
    total = one_term(in_ref[near * PIECE:stride, :])
    for far in range(1, FAR):
        total = total + one_term(in_ref[far * stride + near * PIECE:(far + 1) * stride, :])
    terms = two_terms(total)
    for dest in range(near):
        for slot in range(SLOTS):
            start = pl.multiple_of(place_ref[dest, slot], PIECE)
            out_ref[dest, slot * PIECE:(slot + 1) * PIECE] = in_ref[pl.ds(start, PIECE), :]
        out_ref[dest, SLOTS * PIECE:] = terms


def spread_columns(block, start):
    return [
        jnp.broadcast_to(block[:, at:at + 1], (block.shape[0], 128))
        for at in range(start, start + STRIP)
    ]


def basis_steps(tokens, far, head, in_ref, pivt_ref, factor_ref, coeffs_ref, work_ref, sums_ref):
    rank = pivt_ref.shape[0]
    for source in range(in_ref.shape[0]):
        sums_piece(source, far, sums_ref)[...] = one_term(in_ref[source, SLOTS * PIECE:])
    unfold(head, 1.0 / tokens, sums_ref, work_ref)
    work_ref[:, 384:512] = pivt_ref[...].astype(jnp.float32)
    for first in range(0, rank, PANEL):
        block = work_ref[first:first + PANEL, :]
        for start in range(first, first + PANEL, STRIP):
            following = start + STRIP < first + PANEL
            if start == first:
                columns = spread_columns(block, start)
            for step in range(STRIP):
                if following and step == AHEAD:
                    coming = spread_columns(block, start + STRIP)
                root = lax.rsqrt(columns[step][step:step + 1, :])
                column = columns[step] * root
                for later in range(step + 1, STRIP):
                    columns[later] = columns[later] - column * column[later:later + 1, :]
                if following and step >= AHEAD:
                    for k in range(STRIP):
                        at = STRIP + k
                        coming[k] = coming[k] - column * column[at:at + 1, :]
                line = block[step:step + 1, :] * jnp.concatenate([root] * 4, axis=1)
                work_ref[start + step:start + step + 1, :] = line
                block = block - jnp.concatenate([column] * 4, axis=1) * line
                yield
            if following:
                columns = [one[STRIP:, :] for one in coming]
            block = block[STRIP:, :]
        last = first + PANEL
        if last < rank:
            done = work_ref[first:last, :]
            update = lax.dot_general(
                done[:, 0:rank], done, (((0,), (0,)), ((), ())),
                precision=lax.Precision.HIGHEST, preferred_element_type=jnp.float32,
            )
            work_ref[last:rank, :] = work_ref[last:rank, :] - update[last:rank, :]
    factor_ref[...] = work_ref[:, 256:384]
    coeffs_ref[...] = work_ref[:, 384:512]


def attend_steps(queries_ref, bias_ref, in_ref, kv_ref, out_ref):
    per_dest = SLOTS * PIECE
    half = in_ref.shape[0] // 2
    width = half * per_dest
    keys = jnp.concatenate(
        [in_ref[0:half, 0:per_dest].reshape(width, HD), kv_ref[0:TILE, :]], axis=0
    )
    values = jnp.concatenate(
        [in_ref[half:, 0:per_dest].reshape(width, HD), kv_ref[TILE:, :]], axis=0
    )
    scale = HD ** (-0.5) * math.log2(math.e)
    bias = jnp.concatenate([bias_ref[...]] * TOGETHER, axis=0)
    for first in range(0, GQ, TOGETHER):
        scores = lax.dot_general(
            queries_ref[first * TILE:(first + TOGETHER) * TILE, :], keys,
            (((1,), (1,)), ((), ())), preferred_element_type=jnp.float32,
        ) * scale + bias
        yield
        most = jnp.max(scores, axis=1, keepdims=True)
        yield
        weights = jnp.exp2(scores - most)
        totals = jnp.sum(weights, axis=1, keepdims=True)
        yield
        mixed = jnp.dot(
            weights.astype(jnp.bfloat16), values, preferred_element_type=jnp.float32
        )
        yield
        mixed = (mixed / totals).astype(jnp.bfloat16)
        for g in range(TOGETHER):
            lanes = slice((first + g) * HD, (first + g + 1) * HD)
            out_ref[:, lanes] = mixed[g * TILE:(g + 1) * TILE]


def finish_kernel(
    tokens, far_ref, head_ref, queries_ref, bias_ref, in_ref, kv_ref, pivt_ref,
    out_ref, factor_ref, coeffs_ref, work_ref, sums_ref,
):
    basis = basis_steps(
        tokens, far_ref[0], head_ref[0], in_ref, pivt_ref,
        factor_ref, coeffs_ref, work_ref, sums_ref,
    )
    attend = attend_steps(queries_ref, bias_ref, in_ref, kv_ref, out_ref)
    steps = pivt_ref.shape[0]
    for step in range(steps):
        next(basis, None)
        if step % (steps // (4 * GQ // TOGETHER)) == 0:
            next(attend, None)
    for rest in (attend, basis):
        for _ in rest:
            pass


def on_device(queries, keys, values, tile_mask):
    near_axes = ("x", "near")
    near_size = lax.axis_size(near_axes)
    far_size = lax.axis_size("far")
    head_size = lax.axis_size("head")
    far_index = lax.axis_index("far")
    ctx_index = lax.axis_index(("x", "far", "near"))
    tok_rows = keys.shape[0]
    token_total = tok_rows * near_size * far_size
    rank = head_size * PIVOTS
    positions = ctx_index * tok_rows + lax.iota(jnp.int32, tok_rows)
    cosine, sine = angles(positions.astype(jnp.float32), HD)
    shape = jax.ShapeDtypeStruct
    bf16, f32 = jnp.bfloat16, jnp.float32
    smem, vmem = pl.BlockSpec(memory_space=pltpu.SMEM), pl.BlockSpec(memory_space=pltpu.VMEM)

    def call(kernel, name, out_shape, scalars, *arrays, scratch=()):
        return pl.pallas_call(
            kernel,
            out_shape=out_shape,
            in_specs=[smem] * scalars + [vmem] * (len(arrays) - scalars),
            scratch_shapes=scratch,
            compiler_params=params(),
            name=name,
        )(*arrays)

    pivots = call(pivots_kernel, "pivots", shape((head_size, 32, TILE), bf16), 0, keys)
    pivots = lax.all_to_all(pivots, "head", 0, 0)
    kv = call(
        prepare_kernel, "prepare", shape((2 * TILE, HD), bf16), 0, keys, values, cosine, sine
    )
    stride = near_size * PIECE + 2 * UNIT
    places = call(
        functools.partial(index_kernel, stride), "index",
        shape((near_size, 128), jnp.int32), 1, far_index.reshape(1), tile_mask,
    )
    turned, bias = call(
        queries_kernel, "queries",
        (shape((GQ * TILE, HD), bf16), shape((TILE, (SLOTS + 1) * TILE), f32)), 1,
        ctx_index.reshape(1), tile_mask, queries, cosine, sine,
    )
    far_index = far_index.reshape(1)
    pivots, kv, places, turned, bias, far_index, head_index = lax.optimization_barrier(
        (pivots, kv, places, turned, bias, far_index, lax.axis_index("head").reshape(1))
    )
    first, pivt = call(
        sums_kernel, "sums",
        (shape((near_size, PIECE + 2 * UNIT, HD), bf16), shape((rank, TILE), bf16)), 1,
        far_index, pivots, keys, kv,
        scratch=[pltpu.VMEM((near_size * UNIT, HD), f32)],
    )
    first = lax.all_to_all(first, near_axes, 0, 0)
    second = call(middle_kernel, "middle", shape((far_size, stride, HD), bf16), 0, first)
    groups = [
        [far * NEAR + (group ^ twist(far)) for far in range(FAR)] for group in range(NEAR)
    ]
    second = lax.all_to_all(second, ("far", "near"), 0, 0, axis_index_groups=groups)
    third = call(
        pick_kernel, "pick", shape((near_size, SLOTS * PIECE + 2 * UNIT, HD), bf16), 1,
        places, second.reshape(far_size * stride, HD),
    )
    third = lax.all_to_all(third, near_axes, 0, 0)

    attn_out, key_factor, coeffs = call(
        functools.partial(finish_kernel, float(token_total)), "finish",
        (shape(queries.shape, bf16), shape((rank, HD), f32), shape((rank, TILE), f32)), 2,
        far_index, head_index, turned, bias, third, kv, pivt,
        scratch=[pltpu.VMEM((rank, 512), f32), pltpu.VMEM((near_size * UNIT, HD), f32)],
    )
    return (attn_out, coeffs.T, key_factor)


def solution(mesh):
    ctx_size, head_size = mesh.shape["ctx"], mesh.shape["head"]
    split = jax.sharding.Mesh(
        mesh.devices.reshape(ctx_size // (FAR * NEAR), FAR, NEAR, head_size),
        ("x", "far", "near", "head"),
    )
    ctx = ("x", "far", "near")
    return jax.shard_map(
        on_device,
        mesh=split,
        in_specs=(P(ctx, "head"), P(ctx, "head"), P(ctx, "head"), P("head", None, None)),
        out_specs=(P(ctx, "head"), P(ctx, None), P(None, "head")),
        check_vma=False,
    )
```

```python
import functools
import math

import jax
import jax.numpy as jnp
from jax import lax
from jax.experimental import pallas as pl
from jax.experimental.pallas import tpu as pltpu
from jax.sharding import PartitionSpec as P

HD = 128
GQ = 8
TILE = 128
PIVOTS = 20
NEAR = 4
FAR = 4
PANEL = 80
STRIP = 8
AHEAD = 5
TOGETHER = 2
PIECE = 16
UNIT = 16
SLOTS = 7
NEG = -1e30
ROPE_BASE = 500000.0
VMEM_LIMIT = 48 * 1024 * 1024


def angles(positions, width):
    inverse = jnp.exp(
        -math.log(ROPE_BASE) * 2.0 * jnp.arange(width // 2, dtype=jnp.float32) / width
    )
    turning = positions[:, None] * inverse[None, :]
    cosine, sine = jnp.cos(turning), jnp.sin(turning)
    return (
        jnp.concatenate([cosine, cosine], axis=1),
        jnp.concatenate([-sine, sine], axis=1),
    )


def turn(head_vals, cosine, signed_sine):
    return head_vals * cosine + pltpu.roll(head_vals, HD // 2, 1) * signed_sine


def params():
    return pltpu.CompilerParams(vmem_limit_bytes=VMEM_LIMIT)


def iota(shape, dim):
    return lax.broadcasted_iota(jnp.int32, shape, dim)


def pivots_kernel(keys_ref, piv_ref):
    first = (iota((32, HD), 0) == iota((32, HD), 1)).astype(jnp.bfloat16)
    pivots = lax.dot_general(
        first, keys_ref[...], (((1,), (1,)), ((), ())), preferred_element_type=jnp.float32
    ).astype(jnp.bfloat16)
    for head in range(piv_ref.shape[0]):
        piv_ref[head] = pivots


def prepare_kernel(keys_ref, values_ref, cos_ref, sin_ref, kv_ref):
    keys = keys_ref[...].astype(jnp.float32)
    kv_ref[0:TILE, :] = turn(keys, cos_ref[...], sin_ref[...]).astype(jnp.bfloat16)
    kv_ref[TILE:, :] = values_ref[...]


def queries_kernel(me_ref, mask_ref, queries_ref, cos_ref, sin_ref, out_ref, bias_ref):
    cosine, sine = cos_ref[...], sin_ref[...]
    for g in range(GQ):
        lanes = slice(g * HD, (g + 1) * HD)
        query = turn(queries_ref[:, lanes].astype(jnp.float32), cosine, sine)
        out_ref[g * TILE:(g + 1) * TILE, :] = query.astype(jnp.bfloat16)
    mask = mask_ref[0]
    count = jnp.sum(jnp.where(iota(mask.shape, 0) == me_ref[0], mask, 0)) - 1
    width = SLOTS * TILE
    slot = iota((TILE, width), 1) % (SLOTS * PIECE) // PIECE
    bias_ref[:, 0:width] = jnp.where(slot < count, 0.0, NEG)
    below = iota((TILE, TILE), 1) <= iota((TILE, TILE), 0)
    bias_ref[:, width:] = jnp.where(below, 0.0, NEG)


def index_kernel(stride, far_ref, mask_ref, out_ref):
    tiles = mask_ref.shape[1]
    dests = out_ref.shape[0]
    mask = mask_ref[0].astype(jnp.bfloat16)
    dest = iota((dests, tiles), 0)
    tile = dest // NEAR * FAR * NEAR + far_ref[0] * NEAR + dest % NEAR
    own = (tile == iota((dests, tiles), 1)).astype(jnp.bfloat16)
    mine = jnp.dot(own, mask, preferred_element_type=jnp.float32)
    mine = mine * (1.0 - own.astype(jnp.float32))
    before = (iota((tiles, tiles), 0) < iota((tiles, tiles), 1)).astype(jnp.bfloat16)
    rank = jnp.dot(mine.astype(jnp.bfloat16), before, preferred_element_type=jnp.float32)
    col = iota((dests, tiles), 1)
    place = col // NEAR % FAR * stride + (col // (FAR * NEAR) * NEAR + col % NEAR) * PIECE
    place = place.astype(jnp.float32) * mine
    lane = iota(out_ref.shape, 1)
    found = jnp.zeros(out_ref.shape, jnp.float32)
    for slot in range(SLOTS):
        value = jnp.sum(jnp.where(rank == slot, place, 0.0), axis=1, keepdims=True)
        found = jnp.where(lane == slot, value, found)
    out_ref[...] = found.astype(jnp.int32)


def two_terms(total):
    high = total.astype(jnp.bfloat16).astype(jnp.float32)
    return jnp.concatenate([high, total - high], axis=0).astype(jnp.bfloat16)


def one_term(terms):
    terms = terms.astype(jnp.float32)
    half = terms.shape[0] // 2
    return terms[0:half] + terms[half:]


def fold(cross, gram, all_ref):
    rank, half = gram.shape[0], 64
    rest = rank - 128
    row, lane = iota((half, 128), 0), iota((half, 128), 1)
    low = gram[half:128, 0:128]
    diagonal = jnp.sum(jnp.where(lane == row + half, low, 0.0), axis=1, keepdims=True)
    corner = jnp.concatenate(
        [gram[128:, 128:], jnp.zeros((rest, 128 - rest), jnp.float32)], axis=1
    )
    hidden = jnp.concatenate(
        [
            corner,
            pltpu.roll(corner, 128 - rest // 2, 1),
            jnp.broadcast_to(diagonal, (half, 128)),
            jnp.zeros((rank - 2 * rest - half, 128), jnp.float32),
        ],
        axis=0,
    )
    all_ref[0:rank, :] = jnp.where(iota((rank, 128), 1) < PIVOTS, hidden, cross)
    keep = (lane < half) & (lane <= row)
    all_ref[rank:rank + half, :] = jnp.where(keep, gram[0:half, 0:128], pltpu.roll(low, half, 1))
    all_ref[rank + half:, :] = gram[128:, 0:128]


def unfold(head, inverse, sums_ref, work_ref):
    rank, half = work_ref.shape[0], 64
    rest = rank - 128
    row, lane = iota((half, 128), 0), iota((half, 128), 1)
    mixed = sums_ref[rank:rank + half, :] * inverse
    turned = pltpu.roll(mixed, half, 1)
    diagonal = jnp.broadcast_to(sums_ref[2 * rest:2 * rest + half, 0:1], (half, 128)) * inverse
    top = jnp.where((lane < half) & (lane <= row), mixed, 0.0)
    low = jnp.where(
        (lane < half) | (lane > row + half), turned, jnp.where(lane == row + half, diagonal, 0.0)
    )
    one_side = jnp.concatenate([top, low], axis=0)
    other = jnp.where(iota((128, 128), 0) == iota((128, 128), 1), 0.0, one_side.T)
    work_ref[0:128, 0:128] = one_side + other
    last = sums_ref[rank + half:, :] * inverse
    work_ref[128:, 0:128] = last
    work_ref[0:128, 128:256] = jnp.concatenate(
        [last, jnp.zeros((128 - rest, 128), jnp.float32)], axis=0
    ).T
    lane = iota((rest, 128), 1)
    second = pltpu.roll(sums_ref[rest:2 * rest, :], rest // 2, 1)
    corner = jnp.where(lane < rest // 2, sums_ref[0:rest, :], second)
    work_ref[128:, 128:256] = jnp.where(lane < rest, corner * inverse, 0.0)
    own = pltpu.roll(work_ref[:, 0:256], 256 - head * PIVOTS, 1)[:, 0:128]
    work_ref[:, 256:384] = jnp.where(
        iota((rank, 128), 1) < PIVOTS, own, sums_ref[0:rank, :] * inverse
    )


def twist(far):
    return far // 2 * 2


def sums_piece(index, far, ref):
    return ref.at[pl.ds(pl.multiple_of((index ^ twist(far)) * UNIT, UNIT), UNIT), :]


def sums_kernel(far_ref, piv_ref, keys_ref, kv_ref, out_ref, pivt_ref, all_ref):
    heads = piv_ref.shape[0]
    rank = heads * PIVOTS
    padded = piv_ref[...].reshape(heads * 32, TILE)
    line = iota((rank, heads * 32), 0)
    place = line // PIVOTS * 32 + line % PIVOTS
    compact = (place == iota((rank, heads * 32), 1)).astype(jnp.bfloat16)
    pivt = jnp.dot(compact, padded, preferred_element_type=jnp.float32).astype(jnp.bfloat16)
    pivt_ref[...] = pivt
    cross = jnp.dot(pivt, keys_ref[...], preferred_element_type=jnp.float32)
    gram = lax.dot_general(
        pivt, pivt, (((1,), (1,)), ((), ())), preferred_element_type=jnp.float32
    )
    fold(cross, gram, all_ref)
    for dest in range(out_ref.shape[0]):
        out_ref[dest, 0:PIECE] = kv_ref[dest * PIECE:(dest + 1) * PIECE, :]
        out_ref[dest, PIECE:] = two_terms(sums_piece(dest, far_ref[0], all_ref)[...])


def middle_kernel(in_ref, out_ref):
    near = in_ref.shape[0]
    total = one_term(in_ref[0, PIECE:])
    for source in range(1, near):
        total = total + one_term(in_ref[source, PIECE:])
    terms = two_terms(total)
    for dest in range(out_ref.shape[0]):
        for source in range(near):
            out_ref[dest, source * PIECE:(source + 1) * PIECE] = in_ref[source, 0:PIECE]
        out_ref[dest, near * PIECE:] = terms


def pick_kernel(place_ref, in_ref, out_ref):
    near, stride = out_ref.shape[0], in_ref.shape[0] // FAR
    total = one_term(in_ref[near * PIECE:stride, :])
    for far in range(1, FAR):
        total = total + one_term(in_ref[far * stride + near * PIECE:(far + 1) * stride, :])
    terms = two_terms(total)
    for dest in range(near):
        for slot in range(SLOTS):
            start = pl.multiple_of(place_ref[dest, slot], PIECE)
            out_ref[dest, slot * PIECE:(slot + 1) * PIECE] = in_ref[pl.ds(start, PIECE), :]
        out_ref[dest, SLOTS * PIECE:] = terms


def spread_columns(block, start):
    return [
        jnp.broadcast_to(block[:, at:at + 1], (block.shape[0], 128))
        for at in range(start, start + STRIP)
    ]


def basis_steps(tokens, far, head, in_ref, pivt_ref, factor_ref, coeffs_ref, work_ref, sums_ref):
    rank = pivt_ref.shape[0]
    for source in range(in_ref.shape[0]):
        sums_piece(source, far, sums_ref)[...] = one_term(in_ref[source, SLOTS * PIECE:])
    unfold(head, 1.0 / tokens, sums_ref, work_ref)
    work_ref[:, 384:512] = pivt_ref[...].astype(jnp.float32)
    for first in range(0, rank, PANEL):
        block = work_ref[first:first + PANEL, :]
        for start in range(first, first + PANEL, STRIP):
            following = start + STRIP < first + PANEL
            if start == first:
                columns = spread_columns(block, start)
            for step in range(STRIP):
                if following and step == AHEAD:
                    coming = spread_columns(block, start + STRIP)
                root = lax.rsqrt(columns[step][step:step + 1, :])
                column = columns[step] * root
                for later in range(step + 1, STRIP):
                    columns[later] = columns[later] - column * column[later:later + 1, :]
                if following and step >= AHEAD:
                    for k in range(STRIP):
                        at = STRIP + k
                        coming[k] = coming[k] - column * column[at:at + 1, :]
                line = block[step:step + 1, :] * jnp.concatenate([root] * 4, axis=1)
                work_ref[start + step:start + step + 1, :] = line
                block = block - jnp.concatenate([column] * 4, axis=1) * line
                yield
            if following:
                columns = [one[STRIP:, :] for one in coming]
            block = block[STRIP:, :]
        last = first + PANEL
        if last < rank:
            done = work_ref[first:last, :]
            update = lax.dot_general(
                done[:, 0:rank], done, (((0,), (0,)), ((), ())),
                precision=lax.Precision.HIGHEST, preferred_element_type=jnp.float32,
            )
            work_ref[last:rank, :] = work_ref[last:rank, :] - update[last:rank, :]
    factor_ref[...] = work_ref[:, 256:384]
    coeffs_ref[...] = work_ref[:, 384:512]


def attend_steps(queries_ref, bias_ref, in_ref, kv_ref, out_ref):
    per_dest = SLOTS * PIECE
    half = in_ref.shape[0] // 2
    width = half * per_dest
    keys = jnp.concatenate(
        [in_ref[0:half, 0:per_dest].reshape(width, HD), kv_ref[0:TILE, :]], axis=0
    )
    values = jnp.concatenate(
        [in_ref[half:, 0:per_dest].reshape(width, HD), kv_ref[TILE:, :]], axis=0
    )
    scale = HD ** (-0.5) * math.log2(math.e)
    bias = jnp.concatenate([bias_ref[...]] * TOGETHER, axis=0)
    for first in range(0, GQ, TOGETHER):
        scores = lax.dot_general(
            queries_ref[first * TILE:(first + TOGETHER) * TILE, :], keys,
            (((1,), (1,)), ((), ())), preferred_element_type=jnp.float32,
        ) * scale + bias
        yield
        most = jnp.max(scores, axis=1, keepdims=True)
        yield
        weights = jnp.exp2(scores - most)
        totals = jnp.sum(weights, axis=1, keepdims=True)
        yield
        mixed = jnp.dot(
            weights.astype(jnp.bfloat16), values, preferred_element_type=jnp.float32
        )
        yield
        mixed = (mixed / totals).astype(jnp.bfloat16)
        for g in range(TOGETHER):
            lanes = slice((first + g) * HD, (first + g + 1) * HD)
            out_ref[:, lanes] = mixed[g * TILE:(g + 1) * TILE]


def finish_kernel(
    tokens, far_ref, head_ref, queries_ref, bias_ref, in_ref, kv_ref, pivt_ref,
    out_ref, factor_ref, coeffs_ref, work_ref, sums_ref,
):
    basis = basis_steps(
        tokens, far_ref[0], head_ref[0], in_ref, pivt_ref,
        factor_ref, coeffs_ref, work_ref, sums_ref,
    )
    attend = attend_steps(queries_ref, bias_ref, in_ref, kv_ref, out_ref)
    steps = pivt_ref.shape[0]
    for step in range(steps):
        next(basis, None)
        if step % (steps // (4 * GQ // TOGETHER)) == 0:
            next(attend, None)
    for rest in (attend, basis):
        for _ in rest:
            pass


def on_device(queries, keys, values, tile_mask):
    near_axes = ("x", "near")
    near_size = lax.axis_size(near_axes)
    far_size = lax.axis_size("far")
    head_size = lax.axis_size("head")
    far_index = lax.axis_index("far")
    ctx_index = lax.axis_index(("x", "far", "near"))
    tok_rows = keys.shape[0]
    token_total = tok_rows * near_size * far_size
    rank = head_size * PIVOTS
    positions = ctx_index * tok_rows + lax.iota(jnp.int32, tok_rows)
    cosine, sine = angles(positions.astype(jnp.float32), HD)
    shape = jax.ShapeDtypeStruct
    bf16, f32 = jnp.bfloat16, jnp.float32
    smem, vmem = pl.BlockSpec(memory_space=pltpu.SMEM), pl.BlockSpec(memory_space=pltpu.VMEM)

    def call(kernel, name, out_shape, scalars, *arrays, scratch=()):
        return pl.pallas_call(
            kernel,
            out_shape=out_shape,
            in_specs=[smem] * scalars + [vmem] * (len(arrays) - scalars),
            scratch_shapes=scratch,
            compiler_params=params(),
            name=name,
        )(*arrays)

    pivots = call(pivots_kernel, "pivots", shape((head_size, 32, TILE), bf16), 0, keys)
    pivots = lax.all_to_all(pivots, "head", 0, 0)
    kv = call(
        prepare_kernel, "prepare", shape((2 * TILE, HD), bf16), 0, keys, values, cosine, sine
    )
    stride = near_size * PIECE + 2 * UNIT
    places = call(
        functools.partial(index_kernel, stride), "index",
        shape((near_size, 128), jnp.int32), 1, far_index.reshape(1), tile_mask,
    )
    turned, bias = call(
        queries_kernel, "queries",
        (shape((GQ * TILE, HD), bf16), shape((TILE, (SLOTS + 1) * TILE), f32)), 1,
        ctx_index.reshape(1), tile_mask, queries, cosine, sine,
    )
    far_index = far_index.reshape(1)
    pivots, kv, places, turned, bias, far_index, head_index = lax.optimization_barrier(
        (pivots, kv, places, turned, bias, far_index, lax.axis_index("head").reshape(1))
    )
    first, pivt = call(
        sums_kernel, "sums",
        (shape((near_size, PIECE + 2 * UNIT, HD), bf16), shape((rank, TILE), bf16)), 1,
        far_index, pivots, keys, kv,
        scratch=[pltpu.VMEM((near_size * UNIT, HD), f32)],
    )
    first = lax.all_to_all(first, near_axes, 0, 0)
    second = call(middle_kernel, "middle", shape((far_size, stride, HD), bf16), 0, first)
    groups = [
        [far * NEAR + (group ^ twist(far)) for far in range(FAR)] for group in range(NEAR)
    ]
    second = lax.all_to_all(second, ("far", "near"), 0, 0, axis_index_groups=groups)
    third = call(
        pick_kernel, "pick", shape((near_size, SLOTS * PIECE + 2 * UNIT, HD), bf16), 1,
        places, second.reshape(far_size * stride, HD),
    )
    third = lax.all_to_all(third, near_axes, 0, 0)

    attn_out, key_factor, coeffs = call(
        functools.partial(finish_kernel, float(token_total)), "finish",
        (shape(queries.shape, bf16), shape((rank, HD), f32), shape((rank, TILE), f32)), 2,
        far_index, head_index, turned, bias, third, kv, pivt,
        scratch=[pltpu.VMEM((rank, 512), f32), pltpu.VMEM((near_size * UNIT, HD), f32)],
    )
    return (attn_out, coeffs.T, key_factor)


def solution(mesh):
    ctx_size, head_size = mesh.shape["ctx"], mesh.shape["head"]
    split = jax.sharding.Mesh(
        mesh.devices.reshape(ctx_size // (FAR * NEAR), FAR, NEAR, head_size),
        ("x", "far", "near", "head"),
    )
    ctx = ("x", "far", "near")
    return jax.shard_map(
        on_device,
        mesh=split,
        in_specs=(P(ctx, "head"), P(ctx, "head"), P(ctx, "head"), P("head", None, None)),
        out_specs=(P(ctx, "head"), P(ctx, None), P(None, "head")),
        check_vma=False,
    )
```

```python
import functools
import math

import jax
import jax.numpy as jnp
from jax import lax
from jax.experimental import pallas as pl
from jax.experimental.pallas import tpu as pltpu
from jax.sharding import PartitionSpec as P

HD = 128
GQ = 8
TILE = 128
PIVOTS = 20
NEAR = 4
FAR = 4
PANEL = 40
STRIP = 8
AHEAD = 5
TOGETHER = 4
PIECE = 16
UNIT = 16
SLOTS = 7
NEG = -1e30
ROPE_BASE = 500000.0
VMEM_LIMIT = 48 * 1024 * 1024


def angles(positions, width):
    inverse = jnp.exp(
        -math.log(ROPE_BASE) * 2.0 * jnp.arange(width // 2, dtype=jnp.float32) / width
    )
    turning = positions[:, None] * inverse[None, :]
    cosine, sine = jnp.cos(turning), jnp.sin(turning)
    return (
        jnp.concatenate([cosine, cosine], axis=1),
        jnp.concatenate([-sine, sine], axis=1),
    )


def turn(head_vals, cosine, signed_sine):
    return head_vals * cosine + pltpu.roll(head_vals, HD // 2, 1) * signed_sine


def params():
    return pltpu.CompilerParams(vmem_limit_bytes=VMEM_LIMIT)


def iota(shape, dim):
    return lax.broadcasted_iota(jnp.int32, shape, dim)


def pivots_kernel(keys_ref, piv_ref):
    first = (iota((32, HD), 0) == iota((32, HD), 1)).astype(jnp.bfloat16)
    pivots = lax.dot_general(
        first, keys_ref[...], (((1,), (1,)), ((), ())), preferred_element_type=jnp.float32
    ).astype(jnp.bfloat16)
    for head in range(piv_ref.shape[0]):
        piv_ref[head] = pivots


def prepare_kernel(keys_ref, values_ref, cos_ref, sin_ref, kv_ref):
    keys = keys_ref[...].astype(jnp.float32)
    kv_ref[0:TILE, :] = turn(keys, cos_ref[...], sin_ref[...]).astype(jnp.bfloat16)
    kv_ref[TILE:, :] = values_ref[...]


def queries_kernel(me_ref, mask_ref, queries_ref, cos_ref, sin_ref, out_ref, bias_ref):
    cosine, sine = cos_ref[...], sin_ref[...]
    for g in range(GQ):
        lanes = slice(g * HD, (g + 1) * HD)
        query = turn(queries_ref[:, lanes].astype(jnp.float32), cosine, sine)
        out_ref[g * TILE:(g + 1) * TILE, :] = query.astype(jnp.bfloat16)
    mask = mask_ref[0]
    count = jnp.sum(jnp.where(iota(mask.shape, 0) == me_ref[0], mask, 0)) - 1
    width = SLOTS * TILE
    slot = iota((TILE, width), 1) % (SLOTS * PIECE) // PIECE
    bias_ref[:, 0:width] = jnp.where(slot < count, 0.0, NEG)
    below = iota((TILE, TILE), 1) <= iota((TILE, TILE), 0)
    bias_ref[:, width:] = jnp.where(below, 0.0, NEG)


def index_kernel(stride, far_ref, mask_ref, out_ref):
    tiles = mask_ref.shape[1]
    dests = out_ref.shape[0]
    mask = mask_ref[0].astype(jnp.bfloat16)
    dest = iota((dests, tiles), 0)
    tile = dest // NEAR * FAR * NEAR + far_ref[0] * NEAR + dest % NEAR
    own = (tile == iota((dests, tiles), 1)).astype(jnp.bfloat16)
    mine = jnp.dot(own, mask, preferred_element_type=jnp.float32)
    mine = mine * (1.0 - own.astype(jnp.float32))
    before = (iota((tiles, tiles), 0) < iota((tiles, tiles), 1)).astype(jnp.bfloat16)
    rank = jnp.dot(mine.astype(jnp.bfloat16), before, preferred_element_type=jnp.float32)
    col = iota((dests, tiles), 1)
    place = col // NEAR % FAR * stride + (col // (FAR * NEAR) * NEAR + col % NEAR) * PIECE
    place = place.astype(jnp.float32) * mine
    lane = iota(out_ref.shape, 1)
    found = jnp.zeros(out_ref.shape, jnp.float32)
    for slot in range(SLOTS):
        value = jnp.sum(jnp.where(rank == slot, place, 0.0), axis=1, keepdims=True)
        found = jnp.where(lane == slot, value, found)
    out_ref[...] = found.astype(jnp.int32)


def two_terms(total):
    high = total.astype(jnp.bfloat16).astype(jnp.float32)
    return jnp.concatenate([high, total - high], axis=0).astype(jnp.bfloat16)


def one_term(terms):
    terms = terms.astype(jnp.float32)
    half = terms.shape[0] // 2
    return terms[0:half] + terms[half:]


def fold(cross, gram, all_ref):
    rank, half = gram.shape[0], 64
    rest = rank - 128
    row, lane = iota((half, 128), 0), iota((half, 128), 1)
    low = gram[half:128, 0:128]
    diagonal = jnp.sum(jnp.where(lane == row + half, low, 0.0), axis=1, keepdims=True)
    corner = jnp.concatenate(
        [gram[128:, 128:], jnp.zeros((rest, 128 - rest), jnp.float32)], axis=1
    )
    hidden = jnp.concatenate(
        [
            corner,
            pltpu.roll(corner, 128 - rest // 2, 1),
            jnp.broadcast_to(diagonal, (half, 128)),
            jnp.zeros((rank - 2 * rest - half, 128), jnp.float32),
        ],
        axis=0,
    )
    all_ref[0:rank, :] = jnp.where(iota((rank, 128), 1) < PIVOTS, hidden, cross)
    keep = (lane < half) & (lane <= row)
    all_ref[rank:rank + half, :] = jnp.where(keep, gram[0:half, 0:128], pltpu.roll(low, half, 1))
    all_ref[rank + half:, :] = gram[128:, 0:128]


def unfold(head, inverse, sums_ref, work_ref):
    rank, half = work_ref.shape[0], 64
    rest = rank - 128
    row, lane = iota((half, 128), 0), iota((half, 128), 1)
    mixed = sums_ref[rank:rank + half, :] * inverse
    turned = pltpu.roll(mixed, half, 1)
    diagonal = jnp.broadcast_to(sums_ref[2 * rest:2 * rest + half, 0:1], (half, 128)) * inverse
    top = jnp.where((lane < half) & (lane <= row), mixed, 0.0)
    low = jnp.where(
        (lane < half) | (lane > row + half), turned, jnp.where(lane == row + half, diagonal, 0.0)
    )
    one_side = jnp.concatenate([top, low], axis=0)
    other = jnp.where(iota((128, 128), 0) == iota((128, 128), 1), 0.0, one_side.T)
    work_ref[0:128, 0:128] = one_side + other
    last = sums_ref[rank + half:, :] * inverse
    work_ref[128:, 0:128] = last
    work_ref[0:128, 128:256] = jnp.concatenate(
        [last, jnp.zeros((128 - rest, 128), jnp.float32)], axis=0
    ).T
    lane = iota((rest, 128), 1)
    second = pltpu.roll(sums_ref[rest:2 * rest, :], rest // 2, 1)
    corner = jnp.where(lane < rest // 2, sums_ref[0:rest, :], second)
    work_ref[128:, 128:256] = jnp.where(lane < rest, corner * inverse, 0.0)
    own = pltpu.roll(work_ref[:, 0:256], 256 - head * PIVOTS, 1)[:, 0:128]
    work_ref[:, 256:384] = jnp.where(
        iota((rank, 128), 1) < PIVOTS, own, sums_ref[0:rank, :] * inverse
    )


def twist(far):
    return far // 2 * 2


def sums_piece(index, far, ref):
    return ref.at[pl.ds(pl.multiple_of((index ^ twist(far)) * UNIT, UNIT), UNIT), :]


def sums_kernel(far_ref, piv_ref, keys_ref, kv_ref, out_ref, pivt_ref, all_ref):
    heads = piv_ref.shape[0]
    rank = heads * PIVOTS
    padded = piv_ref[...].reshape(heads * 32, TILE)
    line = iota((rank, heads * 32), 0)
    place = line // PIVOTS * 32 + line % PIVOTS
    compact = (place == iota((rank, heads * 32), 1)).astype(jnp.bfloat16)
    pivt = jnp.dot(compact, padded, preferred_element_type=jnp.float32).astype(jnp.bfloat16)
    pivt_ref[...] = pivt
    cross = jnp.dot(pivt, keys_ref[...], preferred_element_type=jnp.float32)
    gram = lax.dot_general(
        pivt, pivt, (((1,), (1,)), ((), ())), preferred_element_type=jnp.float32
    )
    fold(cross, gram, all_ref)
    for dest in range(out_ref.shape[0]):
        out_ref[dest, 0:PIECE] = kv_ref[dest * PIECE:(dest + 1) * PIECE, :]
        out_ref[dest, PIECE:] = two_terms(sums_piece(dest, far_ref[0], all_ref)[...])


def middle_kernel(in_ref, out_ref):
    near = in_ref.shape[0]
    total = one_term(in_ref[0, PIECE:])
    for source in range(1, near):
        total = total + one_term(in_ref[source, PIECE:])
    terms = two_terms(total)
    for dest in range(out_ref.shape[0]):
        for source in range(near):
            out_ref[dest, source * PIECE:(source + 1) * PIECE] = in_ref[source, 0:PIECE]
        out_ref[dest, near * PIECE:] = terms


def pick_kernel(place_ref, in_ref, out_ref):
    near, stride = out_ref.shape[0], in_ref.shape[0] // FAR
    total = one_term(in_ref[near * PIECE:stride, :])
    for far in range(1, FAR):
        total = total + one_term(in_ref[far * stride + near * PIECE:(far + 1) * stride, :])
    terms = two_terms(total)
    for dest in range(near):
        for slot in range(SLOTS):
            start = pl.multiple_of(place_ref[dest, slot], PIECE)
            out_ref[dest, slot * PIECE:(slot + 1) * PIECE] = in_ref[pl.ds(start, PIECE), :]
        out_ref[dest, SLOTS * PIECE:] = terms


def spread_columns(block, start):
    return [
        jnp.broadcast_to(block[:, at:at + 1], (block.shape[0], 128))
        for at in range(start, start + STRIP)
    ]


def basis_steps(tokens, far, head, in_ref, pivt_ref, factor_ref, coeffs_ref, work_ref, sums_ref):
    rank = pivt_ref.shape[0]
    for source in range(in_ref.shape[0]):
        sums_piece(source, far, sums_ref)[...] = one_term(in_ref[source, SLOTS * PIECE:])
    unfold(head, 1.0 / tokens, sums_ref, work_ref)
    work_ref[:, 384:512] = pivt_ref[...].astype(jnp.float32)
    for first in range(0, rank, PANEL):
        block = work_ref[first:first + PANEL, :]
        for start in range(first, first + PANEL, STRIP):
            following = start + STRIP < first + PANEL
            if start == first:
                columns = spread_columns(block, start)
            for step in range(STRIP):
                if following and step == AHEAD:
                    coming = spread_columns(block, start + STRIP)
                root = lax.rsqrt(columns[step][step:step + 1, :])
                column = columns[step] * root
                for later in range(step + 1, STRIP):
                    columns[later] = columns[later] - column * column[later:later + 1, :]
                if following and step >= AHEAD:
                    for k in range(STRIP):
                        at = STRIP + k
                        coming[k] = coming[k] - column * column[at:at + 1, :]
                line = block[step:step + 1, :] * jnp.concatenate([root] * 4, axis=1)
                work_ref[start + step:start + step + 1, :] = line
                block = block - jnp.concatenate([column] * 4, axis=1) * line
                yield
            if following:
                columns = [one[STRIP:, :] for one in coming]
            block = block[STRIP:, :]
        last = first + PANEL
        if last < rank:
            done = work_ref[first:last, :]
            update = lax.dot_general(
                done[:, 0:rank], done, (((0,), (0,)), ((), ())),
                precision=lax.Precision.HIGHEST, preferred_element_type=jnp.float32,
            )
            work_ref[last:rank, :] = work_ref[last:rank, :] - update[last:rank, :]
    factor_ref[...] = work_ref[:, 256:384]
    coeffs_ref[...] = work_ref[:, 384:512]


def attend_steps(queries_ref, bias_ref, in_ref, kv_ref, out_ref):
    per_dest = SLOTS * PIECE
    half = in_ref.shape[0] // 2
    width = half * per_dest
    keys = jnp.concatenate(
        [in_ref[0:half, 0:per_dest].reshape(width, HD), kv_ref[0:TILE, :]], axis=0
    )
    values = jnp.concatenate(
        [in_ref[half:, 0:per_dest].reshape(width, HD), kv_ref[TILE:, :]], axis=0
    )
    scale = HD ** (-0.5) * math.log2(math.e)
    bias = jnp.concatenate([bias_ref[...]] * TOGETHER, axis=0)
    for first in range(0, GQ, TOGETHER):
        scores = lax.dot_general(
            queries_ref[first * TILE:(first + TOGETHER) * TILE, :], keys,
            (((1,), (1,)), ((), ())), preferred_element_type=jnp.float32,
        ) * scale + bias
        yield
        most = jnp.max(scores, axis=1, keepdims=True)
        yield
        weights = jnp.exp2(scores - most)
        totals = jnp.sum(weights, axis=1, keepdims=True)
        yield
        mixed = jnp.dot(
            weights.astype(jnp.bfloat16), values, preferred_element_type=jnp.float32
        )
        yield
        mixed = (mixed / totals).astype(jnp.bfloat16)
        for g in range(TOGETHER):
            lanes = slice((first + g) * HD, (first + g + 1) * HD)
            out_ref[:, lanes] = mixed[g * TILE:(g + 1) * TILE]


def finish_kernel(
    tokens, far_ref, head_ref, queries_ref, bias_ref, in_ref, kv_ref, pivt_ref,
    out_ref, factor_ref, coeffs_ref, work_ref, sums_ref,
):
    basis = basis_steps(
        tokens, far_ref[0], head_ref[0], in_ref, pivt_ref,
        factor_ref, coeffs_ref, work_ref, sums_ref,
    )
    attend = attend_steps(queries_ref, bias_ref, in_ref, kv_ref, out_ref)
    steps = pivt_ref.shape[0]
    for step in range(steps):
        next(basis, None)
        if step % (steps // (4 * GQ // TOGETHER)) == 0:
            next(attend, None)
    for rest in (attend, basis):
        for _ in rest:
            pass


def on_device(queries, keys, values, tile_mask):
    near_axes = ("x", "near")
    near_size = lax.axis_size(near_axes)
    far_size = lax.axis_size("far")
    head_size = lax.axis_size("head")
    far_index = lax.axis_index("far")
    ctx_index = lax.axis_index(("x", "far", "near"))
    tok_rows = keys.shape[0]
    token_total = tok_rows * near_size * far_size
    rank = head_size * PIVOTS
    positions = ctx_index * tok_rows + lax.iota(jnp.int32, tok_rows)
    cosine, sine = angles(positions.astype(jnp.float32), HD)
    shape = jax.ShapeDtypeStruct
    bf16, f32 = jnp.bfloat16, jnp.float32
    smem, vmem = pl.BlockSpec(memory_space=pltpu.SMEM), pl.BlockSpec(memory_space=pltpu.VMEM)

    def call(kernel, name, out_shape, scalars, *arrays, scratch=()):
        return pl.pallas_call(
            kernel,
            out_shape=out_shape,
            in_specs=[smem] * scalars + [vmem] * (len(arrays) - scalars),
            scratch_shapes=scratch,
            compiler_params=params(),
            name=name,
        )(*arrays)

    pivots = call(pivots_kernel, "pivots", shape((head_size, 32, TILE), bf16), 0, keys)
    pivots = lax.all_to_all(pivots, "head", 0, 0)
    kv = call(
        prepare_kernel, "prepare", shape((2 * TILE, HD), bf16), 0, keys, values, cosine, sine
    )
    stride = near_size * PIECE + 2 * UNIT
    places = call(
        functools.partial(index_kernel, stride), "index",
        shape((near_size, 128), jnp.int32), 1, far_index.reshape(1), tile_mask,
    )
    turned, bias = call(
        queries_kernel, "queries",
        (shape((GQ * TILE, HD), bf16), shape((TILE, (SLOTS + 1) * TILE), f32)), 1,
        ctx_index.reshape(1), tile_mask, queries, cosine, sine,
    )
    far_index = far_index.reshape(1)
    pivots, kv, places, turned, bias, far_index, head_index = lax.optimization_barrier(
        (pivots, kv, places, turned, bias, far_index, lax.axis_index("head").reshape(1))
    )
    first, pivt = call(
        sums_kernel, "sums",
        (shape((near_size, PIECE + 2 * UNIT, HD), bf16), shape((rank, TILE), bf16)), 1,
        far_index, pivots, keys, kv,
        scratch=[pltpu.VMEM((near_size * UNIT, HD), f32)],
    )
    first = lax.all_to_all(first, near_axes, 0, 0)
    second = call(middle_kernel, "middle", shape((far_size, stride, HD), bf16), 0, first)
    groups = [
        [far * NEAR + (group ^ twist(far)) for far in range(FAR)] for group in range(NEAR)
    ]
    second = lax.all_to_all(second, ("far", "near"), 0, 0, axis_index_groups=groups)
    third = call(
        pick_kernel, "pick", shape((near_size, SLOTS * PIECE + 2 * UNIT, HD), bf16), 1,
        places, second.reshape(far_size * stride, HD),
    )
    third = lax.all_to_all(third, near_axes, 0, 0)

    attn_out, key_factor, coeffs = call(
        functools.partial(finish_kernel, float(token_total)), "finish",
        (shape(queries.shape, bf16), shape((rank, HD), f32), shape((rank, TILE), f32)), 2,
        far_index, head_index, turned, bias, third, kv, pivt,
        scratch=[pltpu.VMEM((rank, 512), f32), pltpu.VMEM((near_size * UNIT, HD), f32)],
    )
    return (attn_out, coeffs.T, key_factor)


def solution(mesh):
    ctx_size, head_size = mesh.shape["ctx"], mesh.shape["head"]
    split = jax.sharding.Mesh(
        mesh.devices.reshape(ctx_size // (FAR * NEAR), FAR, NEAR, head_size),
        ("x", "far", "near", "head"),
    )
    ctx = ("x", "far", "near")
    return jax.shard_map(
        on_device,
        mesh=split,
        in_specs=(P(ctx, "head"), P(ctx, "head"), P(ctx, "head"), P("head", None, None)),
        out_specs=(P(ctx, "head"), P(ctx, None), P(None, "head")),
        check_vma=False,
    )
```
